128 devices in a mesh: spec: 16 (over y, z), space: 8 (over x, core).
Axes of the slice: x: 4, y: 4, z: 4, core: 2. Of those that a mesh axis runs over, the one named last changes fastest.
Arguments:
- spectrum: float32 [576, 256, 512], P('spec', 'space'), may hold values from 0.05 to 18
- land_mask: int32 [256, 512], P('space'), may hold values from 0 to 1, as said below
- celerity: float32 [256, 512], P('space'), may hold values from 0.5 to 1
- turning: float32 [256, 512], P('space'), may hold values from -0.45 to 0.45
- wind_speed: float32 [256, 512], P('space'), may hold values from 0.25 to 2.5
- wind_dir: float32 [256, 512], P('space'), may hold values from -3.140625 to 3.140625
- tile_order: int32 [1024], replicated, may hold values from 0 to 1023, as said below
Outputs:
- spectrum_next: float32 [576, 256, 512], P('spec', 'space')
- tile_spectra: float32 [1024, 576, 128], P(('spec', 'space'))
The draws below stay inside these ranges and needn't reach their ends.
Inputs may be any that keep to these rules, and one draw needn't show every extreme that they name: `land_mask`: 1 marks a sea cell, 0 land. `tile_order`: a permutation of the 1024 tiles; slot q belongs to device q // 8, devices counted along spec then space; every device owns exactly one tile of each row band of 32 rows.
All inputs are finite; a program needn't handle non-finite values.
Results may differ from the reference program's by a relative error of at most 0.00002.
Values sent between devices are 32-bit elements; how exact they have to be, the bound alone decides.
No kernel may reach another device: no remote copies, remote signals or barrier semaphores. Data moves between devices by JAX's collectives and lax.ppermute only.
A program may use at most 64 MiB of HBM per device.

```python
import math
import jax
import jax.numpy as jnp
from jax import lax

NDIR = 36
NFREQ = 16
NBINS = 576
RX = 32
NY = 512
NX = 256
TY = 128
TX = 1
TILES = 1024
PROP_STEPS = 2
N_SPACE = 8
DEVICES = 128


def sea_cells(key):
    tile_rows = NX // TX
    tile_cols = NY // TY
    threshold = jax.random.randint(jax.random.fold_in(key, 11), (tile_rows, tile_cols), 0, 7)
    cells = jax.random.randint(jax.random.fold_in(key, 12), (tile_rows, TX, tile_cols, TY), 0, 8)
    marked = (cells >= threshold[:, None, :, None]).astype(jnp.int32)
    return marked.reshape(NX, NY)


def draw_spectrum(key, part):
    key = jax.random.fold_in(key, 5)
    level = ((jnp.arange(NBINS, dtype=jnp.int32) // NDIR).astype(jnp.float32) / (NFREQ - 1)).reshape(NBINS, 1, 1)
    base = jnp.exp(jax.random.uniform(key, (NBINS, NX, NY), jnp.float32, math.log(0.05), math.log(2.0)))
    scale = jnp.exp(level * math.log(3.0))
    return base * scale


def draw_land_mask(key, part):
    marked = sea_cells(key)
    return marked


def draw_tile_order(key, part):
    marked = sea_cells(key)
    tile_rows = NX // TX
    tile_cols = NY // TY
    per_band = RX // TX * tile_cols
    per_device = TILES // DEVICES
    stride = max(1, N_SPACE // per_device)
    counts = marked.reshape(tile_rows, TX, tile_cols, TY).sum(axis=(1, 3)).reshape(N_SPACE, per_band)
    heavy_first = jnp.argsort(-counts, axis=1, stable=True).astype(jnp.int32)
    slot_index = jnp.arange(TILES, dtype=jnp.int32)
    device_of = slot_index // per_device
    within = slot_index % per_device
    band_of = (device_of + within * stride) % N_SPACE
    onehot = (band_of[:, None] == jnp.arange(N_SPACE, dtype=jnp.int32)[None, :]).astype(jnp.int32)
    position = jnp.sum(jnp.cumsum(onehot, axis=0) * onehot, axis=1) - 1
    chosen = jnp.where(position % 2 == 0, position // 2, per_band - 1 - position // 2)
    return (band_of * per_band + heavy_first[band_of, chosen]).astype(jnp.int32)


def steps_of(key, dims, cuts, least, top_value):
    def one(axis_at, parts):
        heights = jax.random.uniform(jax.random.fold_in(jax.random.fold_in(key, 6), axis_at), (parts,), jnp.float32, least / len(cuts), top_value / len(cuts))
        return jnp.repeat(jnp.exp(heights), dims[axis_at] // parts).reshape((-1,) + (1,) * (len(dims) - axis_at - 1))

    loudness = one(*cuts[0])
    for cut in cuts[1:]:
        loudness = loudness * one(*cut)
    return loudness


def setup_inputs(seed: int = 0) -> dict:
    streams_of = jax.random.split(jax.random.key(seed), 8)
    return {
        "spectrum": draw_spectrum(jax.random.fold_in(streams_of[7], 71), 0),
        "land_mask": draw_land_mask(jax.random.fold_in(streams_of[7], 71), 0),
        "celerity": jnp.clip(0.5 + 0.5 * jax.random.uniform(streams_of[2], (NX, NY), jnp.float32) ** steps_of(streams_of[2], (NX, NY), ((0, 8),), -0.2, 0.2), 0.5, 1.0),
        "turning": jnp.clip(jax.random.uniform(streams_of[3], (NX, NY), jnp.float32, -0.45, 0.45) * steps_of(streams_of[3], (NX, NY), ((0, 8),), -0.4, 0.0), -0.45, 0.45),
        "wind_speed": jnp.clip(jnp.exp(math.log(2.5) - 2.3025851 * jax.random.uniform(streams_of[4], (NX, NY), jnp.float32) ** steps_of(streams_of[4], (NX, NY), ((0, 8),), -0.2, 0.2)), 0.25, 2.5),
        "wind_dir": jnp.clip(jax.random.uniform(streams_of[5], (NX, NY), jnp.float32, -3.140625, 3.140625), -3.140625, 3.140625),
        "tile_order": draw_tile_order(jax.random.fold_in(streams_of[7], 71), 0),
    }


FREQ_RATIO = 1.1
COURANT = 0.45


def group_speeds(first, count):
    freq_index = first + jnp.arange(count, dtype=jnp.int32)
    return jnp.exp(-freq_index.astype(jnp.float32) * math.log(FREQ_RATIO))


def bin_coefficients(first, count, dir_count):
    bin_index = first + jnp.arange(count, dtype=jnp.int32)
    freq_index = bin_index // dir_count
    bin_angle = ((bin_index % dir_count).astype(jnp.float32) + 0.5) * (2.0 * math.pi / dir_count)
    speed = jnp.exp(-freq_index.astype(jnp.float32) * math.log(FREQ_RATIO))
    return COURANT * speed * jnp.cos(bin_angle), COURANT * speed * jnp.sin(bin_angle)


def update(energy, flux_x_ext, flux_y, wet_cells):
    flux_x = flux_x_ext[..., 1:-1, :]
    from_rows = jnp.maximum(flux_x_ext[..., :-2, :], 0.0) + jnp.maximum(-flux_x_ext[..., 2:, :], 0.0)
    zero_col = jnp.zeros_like(flux_y[..., :1])
    from_left = jnp.concatenate([zero_col, flux_y[..., :-1]], axis=-1)
    from_right = jnp.concatenate([flux_y[..., 1:], zero_col], axis=-1)
    from_cols = jnp.maximum(from_left, 0.0) + jnp.maximum(-from_right, 0.0)
    return wet_cells * (energy - jnp.abs(flux_x) - jnp.abs(flux_y) + from_rows + from_cols)


def refract(energy, turning, first_freq):
    layers, freq_count, dir_count, cells = energy.shape
    speed = group_speeds(first_freq, freq_count).reshape(1, freq_count, 1, 1)
    dir_flux = turning[:, None, None, :] * speed * energy
    gained = jnp.maximum(jnp.roll(dir_flux, 1, axis=2), 0.0) + jnp.maximum(-jnp.roll(dir_flux, -1, axis=2), 0.0)
    return energy - jnp.abs(dir_flux) + gained


def grow(refracted, mean_e, wet_cells, wind_speed, wind_dir, first_freq):
    layers, freq_count, dir_count, cells = refracted.shape
    speed = group_speeds(first_freq, freq_count).reshape(1, freq_count, 1, 1)
    bin_angle = ((jnp.arange(dir_count).astype(jnp.float32) + 0.5) * (2.0 * math.pi / dir_count)).reshape(1, 1, dir_count, 1)
    cosine = jnp.cos(bin_angle - wind_dir[:, None, None, :])
    spread = jnp.maximum(cosine, 0.0) ** 2
    wind_force = wind_speed[:, None, None, :]
    grown_energy = refracted * (1.0 + 0.3 * speed * wind_force * spread) + 0.05 * wind_force * wind_force * spread
    damping = 1.0 + 2.0 * speed * speed * mean_e / (1.0 + mean_e)
    return wet_cells[:, None, None, :] * grown_energy / damping


def source(spectra, wet_cells, turning, wind_speed, wind_dir):
    layers, bin_count, cells = spectra.shape
    freq_count = bin_count // NDIR
    energy = spectra.reshape(layers, freq_count, NDIR, cells)
    refracted = refract(energy, turning, 0)
    mean_e = jnp.mean(refracted, axis=(1, 2), keepdims=True)
    return grow(refracted, mean_e, wet_cells, wind_speed, wind_dir, 0).reshape(layers, bin_count, cells)


def reference(spectrum, land_mask, celerity, turning, wind_speed, wind_dir, tile_order):
    wet_cells = land_mask.astype(jnp.float32)
    cel_wet = celerity * wet_cells
    bin_count = spectrum.shape[0]
    coef_x, coef_y = bin_coefficients(0, bin_count, NDIR)

    def advance(payload):
        energy, along_x, along_y = payload
        for substep in range(PROP_STEPS):
            flux_x = along_x * cel_wet * energy
            flux_y = along_y * cel_wet * energy
            padded = jnp.pad(flux_x, ((1, 1), (0, 0)))
            energy = update(energy, padded, flux_y, wet_cells)
        return energy

    propagated = lax.map(advance, (spectrum, coef_x, coef_y))
    band_count = NX // RX
    blocks = propagated.reshape(bin_count, band_count, RX * NY).transpose(1, 0, 2)

    def apply_source(payload):
        spectra, wet_rows, turn_rows, speed_rows, angle_rows = payload
        return source(spectra[None], wet_rows[None], turn_rows[None], speed_rows[None], angle_rows[None])[0]

    forcing_rows = tuple(field.reshape(band_count, RX * NY) for field in (wet_cells, turning, wind_speed, wind_dir))
    finished = lax.map(apply_source, (blocks,) + forcing_rows)
    spectrum_next = finished.transpose(1, 0, 2).reshape(bin_count, NX, NY)
    tile_grid = spectrum_next.reshape(bin_count, NX // TX, TX, NY // TY, TY).transpose(1, 3, 0, 2, 4).reshape(TILES, bin_count, TX * TY)
    tile_spectra = tile_grid[tile_order]
    return spectrum_next, tile_spectra
```

```python
import math

import jax
import jax.numpy as jnp
import numpy as np
from jax import lax
from jax.experimental import pallas as pl
from jax.experimental.pallas import tpu as pltpu
from jax.sharding import PartitionSpec as P

NDIR = 36
NFREQ = 16
NBINS = NDIR * NFREQ
ROWS = 32
COLS = 512
LANES = 128
LTILES = COLS // LANES
STILES = ROWS // 8
DEVICES = 128
OWN = 8
SLOT = NDIR + 1
QUARTER = NDIR // 4
HALF = NDIR // 2
PLANE = NDIR * ROWS

THETA = [2.0 * math.pi * (k + 0.5) / NDIR for k in range(NDIR)]
COS = [float(np.float32(math.cos(t))) for t in THETA]
SIN = [float(np.float32(math.sin(t))) for t in THETA]
SPEED = np.array([1.1 ** (-i) for i in range(NFREQ)], np.float32)
ADVECT = np.array([[0.45 * abs(math.cos(t)) for t in THETA], [0.45 * abs(math.sin(t)) for t in THETA]], np.float32)
QUADRANTS = ((0, 1, 1), (QUARTER, -1, 1), (2 * QUARTER, -1, -1), (3 * QUARTER, 1, -1))

VMEM = pltpu.CompilerParams(vmem_limit_bytes=48 * 1024 * 1024)


def spec_smem():
    return pl.BlockSpec(memory_space=pltpu.SMEM)


def column_shift(tiles, sign, lane):
    edge = 0 if sign > 0 else LANES - 1
    turned = [pltpu.roll(t, 1 if sign > 0 else LANES - 1, 1) for t in tiles]
    zero = jnp.zeros_like(tiles[0])
    out = []
    for j in range(len(tiles)):
        at = j - sign
        out.append(jnp.where(lane == edge, turned[at] if 0 <= at < len(tiles) else zero, turned[j]))
    return out


def row_shift(tiles, sign, sub, halo):
    edge = 0 if sign > 0 else 7
    turned = [pltpu.roll(t, 1 if sign > 0 else 7, 0) for t in tiles]
    out = []
    for i in range(len(tiles)):
        at = i - sign
        out.append(jnp.where(sub == edge, turned[at] if 0 <= at < len(tiles) else halo, turned[i]))
    return out


def advance(energy, flux, ax, ay, sx, sy, sub, lane, halo):
    n = len(energy)
    by_col = [column_shift(flux[i], sy, lane) for i in range(n)]
    total = ax + ay
    out = [[None] * LTILES for _ in range(n)]
    for j in range(LTILES):
        by_row = row_shift([flux[i][j] for i in range(n)], sx, sub, halo[j])
        for i in range(n):
            out[i][j] = energy[i][j] - total * flux[i][j] + ax * by_row[i] + ay * by_col[i][j]
    return out


def iotas():
    return (lax.broadcasted_iota(jnp.int32, (8, LANES), 0), lax.broadcasted_iota(jnp.int32, (8, LANES), 1))


def edge_kernel(at_ref, speed_ref, adv_ref, top_ref, bot_ref, celt_ref, celb_ref, mt_ref, mb_ref, down_ref, up_ref):
    sub, lane = iotas()
    speed = speed_ref[at_ref[0]]
    for first, sx, sy in QUADRANTS:
        src, cel, mask, out, row = (
            (bot_ref, celb_ref, mb_ref, down_ref, 7) if sx > 0 else (top_ref, celt_ref, mt_ref, up_ref, 0)
        )
        cw = [cel[:, pl.ds(j * LANES, LANES)] * mask[:, pl.ds(j * LANES, LANES)].astype(jnp.float32) for j in range(LTILES)]
        zero = [jnp.zeros((8, LANES), jnp.float32)] * LTILES
        at0 = (first + QUARTER) % NDIR if sx > 0 else first - QUARTER

        def body(i, carry):
            k = first + i
            ax = speed * adv_ref[0, k]
            ay = speed * adv_ref[1, k]
            energy = [src[k, :, pl.ds(j * LANES, LANES)] for j in range(LTILES)]
            flux = [cw[j] * energy[j] for j in range(LTILES)]
            after = advance([energy], [flux], ax, ay, sx, sy, sub, lane, zero)[0]
            for j in range(LTILES):
                out[pl.ds(j * NDIR + at0 + i, 1), :] = flux[j][row : row + 1]
                out[pl.ds(j * NDIR + HALF + at0 + i, 1), :] = (cw[j] * after[j])[row : row + 1]
            return carry

        lax.fori_loop(0, QUARTER, body, 0)


def main_kernel(
    at_ref, speed_ref, adv_ref, picked_ref, e_ref, cel_ref, mask_ref, turn_ref, wind_ref, angle_ref, above_ref, below_ref,
    send_ref, grown_ref, sum_ref, e2_ref, cw_ref,
):
    sub, lane = iotas()
    speed = speed_ref[at_ref[0]]
    cw_ref[...] = cel_ref[...] * mask_ref[...].astype(jnp.float32)

    for first, sx, sy in QUADRANTS:
        halo_ref = above_ref if sx > 0 else below_ref
        at0 = (first + QUARTER) % NDIR if sx > 0 else first - QUARTER

        def body(i, carry):
            k = first + i
            ax = speed * adv_ref[0, k]
            ay = speed * adv_ref[1, k]
            cw = [[cw_ref[pl.ds(8 * r, 8), pl.ds(j * LANES, LANES)] for j in range(LTILES)] for r in range(STILES)]
            energy = [[e_ref[k, pl.ds(8 * r, 8), pl.ds(j * LANES, LANES)] for j in range(LTILES)] for r in range(STILES)]
            for step in range(2):
                halo = [
                    jnp.broadcast_to(halo_ref[pl.ds(j * NDIR + step * HALF + at0 + i, 1), :], (8, LANES))
                    for j in range(LTILES)
                ]
                flux = [[cw[r][j] * energy[r][j] for j in range(LTILES)] for r in range(STILES)]
                energy = advance(energy, flux, ax, ay, sx, sy, sub, lane, halo)
            for r in range(STILES):
                for j in range(LTILES):
                    e2_ref[j, pl.ds(pl.multiple_of(k * ROWS, 8) + 8 * r, 8), :] = energy[r][j]
            return carry

        lax.fori_loop(0, QUARTER, body, 0)

    def grow(j, carry):
        cols = pl.ds(pl.multiple_of(j * LANES, LANES), LANES)
        wet = mask_ref[:, cols].astype(jnp.float32)
        turn = turn_ref[:, cols] * speed
        wind = wind_ref[:, cols]
        angle = angle_ref[:, cols]
        stay = wet * (1.0 - jnp.abs(turn))
        from_low = wet * jnp.maximum(turn, 0.0)
        from_high = wet * jnp.maximum(-turn, 0.0)
        cosine = jnp.cos(angle)
        sine = jnp.sin(angle)
        gain = (0.3 * speed) * wind
        force = wet * 0.05 * wind * wind

        def load(k):
            return e2_ref[j, pl.ds((k % NDIR) * ROWS, ROWS), :]

        low, here = load(NDIR - 1), load(0)
        total = jnp.zeros((ROWS, LANES), jnp.float32)
        for k in range(NDIR):
            high = load(k + 1)
            refracted = here * stay + low * from_low + high * from_high
            total = total + refracted
            s = jnp.maximum(cosine * COS[k] + sine * SIN[k], 0.0)
            s = s * s
            grown_ref[j, pl.ds(k * ROWS, ROWS), :] = refracted * (1.0 + gain * s) + force * s
            low, here = here, high
        sum_ref[j] = total
        return carry

    lax.fori_loop(0, LTILES, grow, 0)

    def pack(g, carry):
        base = pl.multiple_of(g * (8 * SLOT), 8)
        for d in range(8):
            tile = picked_ref[g * 8 + d]
            row, col = tile // LTILES, tile % LTILES
            at = base + d * SLOT
            for b in range(0, NDIR, 8):
                n = min(8, NDIR - b)
                send_ref[pl.ds(at + b, n), :] = grown_ref[col, pl.ds(b * ROWS + row, n, stride=ROWS), :]
            send_ref[pl.ds(at + NDIR, 1), :] = sum_ref[col, pl.ds(row, 1), :]
        return carry

    lax.fori_loop(0, DEVICES // 8, pack, 0)


def home_kernel(at_ref, speed_ref, grown_ref, *refs):
    sums, out_ref = refs[:-1], refs[-1]
    speed = speed_ref[at_ref[0]]
    for j in range(LTILES):
        total = sums[0][j]
        for ref in sums[1:]:
            total = total + ref[j]
        mean = total * (1.0 / NBINS)
        scale = 1.0 / (1.0 + (2.0 * speed * speed) * mean / (1.0 + mean))
        for k in range(out_ref.shape[0]):
            out_ref[k, :, pl.ds(j * LANES, LANES)] = grown_ref[j, pl.ds(k * ROWS, ROWS), :] * scale


def owner_kernel(slots_ref, factor_ref, got_ref, out_ref, scale_ref):
    for b in range(OWN):
        q = slots_ref[b]
        sums = got_ref[pl.ds(b * SLOT + NDIR, NFREQ, stride=OWN * SLOT), :]
        mean = jnp.sum(sums, axis=0, keepdims=True) * (1.0 / NBINS)
        scale_ref[...] = 1.0 / (1.0 + factor_ref[...] * mean / (1.0 + mean))

        def body(h, carry):
            for half in range(2):
                s = 2 * h + half
                at = pl.multiple_of(h * (2 * OWN * SLOT), 8) + (half * OWN + b) * SLOT
                to = pl.multiple_of(h * (2 * NDIR), 8) + half * NDIR
                out_ref[q, pl.ds(to, NDIR), :] = got_ref[pl.ds(at, NDIR), :] * scale_ref[pl.ds(s, 1), :]
            return carry

        lax.fori_loop(0, NFREQ // 2, body, 0)


def shards(spectrum, land_mask, celerity, turning, wind_speed, wind_dir, tile_order):
    band = lax.axis_index("space")
    me = lax.axis_index(("spec", "space"))
    at = lax.axis_index("spec").astype(jnp.int32).reshape(1)
    speeds = jnp.asarray(SPEED)
    advect = jnp.asarray(ADVECT)
    space_count = lax.axis_size("space")
    f32 = jnp.float32

    edge = lambda row: pl.BlockSpec((NDIR, 8, COLS), lambda i: (0, row, 0))
    flat = lambda row: pl.BlockSpec((8, COLS), lambda i: (row, 0))
    last = ROWS // 8 - 1
    down, up = pl.pallas_call(
        edge_kernel,
        out_shape=(jax.ShapeDtypeStruct((LTILES * NDIR, LANES), f32),) * 2,
        grid=(1,),
        out_specs=(pl.BlockSpec((LTILES * NDIR, LANES), lambda i: (0, 0)),) * 2,
        in_specs=[spec_smem()] * 3 + [edge(0), edge(last), flat(0), flat(last), flat(0), flat(last)],
        compiler_params=VMEM,
        name="edges",
    )(at, speeds, advect, spectrum, spectrum, celerity, celerity, land_mask, land_mask)
    above = lax.ppermute(down, "space", [(i, i + 1) for i in range(space_count - 1)])
    below = lax.ppermute(up, "space", [(i + 1, i) for i in range(space_count - 1)])

    per_band = ROWS * LTILES
    order = tile_order.reshape(DEVICES, OWN)
    picked = jnp.sum(jnp.where(order // per_band == band, order % per_band, 0), axis=1).astype(jnp.int32)
    own = lax.dynamic_slice_in_dim(order, me, 1, 0).reshape(OWN) // per_band
    slots = jnp.sum(
        jnp.where(own[None, :] == jnp.arange(OWN)[:, None], jnp.arange(OWN)[None, :], 0), axis=1
    ).astype(jnp.int32)

    vmem = pl.BlockSpec(memory_space=pltpu.VMEM)
    send, grown, sums = pl.pallas_call(
        main_kernel,
        out_shape=(
            jax.ShapeDtypeStruct((DEVICES * SLOT, LANES), f32),
            jax.ShapeDtypeStruct((LTILES, PLANE, LANES), f32),
            jax.ShapeDtypeStruct((LTILES, ROWS, LANES), f32),
        ),
        in_specs=[spec_smem()] * 4 + [vmem] * 8,
        out_specs=(vmem,) * 3,
        scratch_shapes=[pltpu.VMEM((LTILES, PLANE, LANES), f32), pltpu.VMEM((ROWS, COLS), f32)],
        compiler_params=VMEM,
        name="bins",
    )(at, speeds, advect, picked, spectrum, celerity, land_mask, turning, wind_speed, wind_dir, above, below)

    got = lax.all_to_all(
        send.reshape(DEVICES, SLOT, 1, LANES), ("spec", "space"), split_axis=0, concat_axis=0, tiled=True
    ).reshape(DEVICES * SLOT, LANES)

    spec_count = lax.axis_size("spec")
    parts = [lax.ppermute(sums, "spec", [(i, i ^ (4 * n)) for i in range(spec_count)]) for n in range(1, 4)]
    fours = sums + parts[0] + parts[1] + parts[2]
    others = [lax.ppermute(fours, "spec", [(i, i ^ n) for i in range(spec_count)]) for n in range(1, 4)]

    chunk = 6
    whole = pl.BlockSpec((LTILES, ROWS, LANES), lambda k: (0, 0, 0))
    spectrum_next = pl.pallas_call(
        home_kernel,
        out_shape=jax.ShapeDtypeStruct((NDIR, ROWS, COLS), f32),
        grid=(NDIR // chunk,),
        in_specs=[spec_smem()] * 2
        + [pl.BlockSpec((LTILES, chunk * ROWS, LANES), lambda k: (0, k, 0))]
        + [whole] * 4,
        out_specs=pl.BlockSpec((chunk, ROWS, COLS), lambda k: (k, 0, 0)),
        compiler_params=VMEM,
        name="home",
    )(at, speeds, grown, fours, *others)

    factor = jnp.broadcast_to(jnp.asarray(2.0 * SPEED * SPEED, f32)[:, None], (NFREQ, LANES))
    tile_spectra = pl.pallas_call(
        owner_kernel,
        out_shape=jax.ShapeDtypeStruct((OWN, NBINS, LANES), f32),
        in_specs=[spec_smem(), vmem, vmem],
        out_specs=vmem,
        scratch_shapes=[pltpu.VMEM((NFREQ, LANES), f32)],
        compiler_params=VMEM,
        name="owned",
    )(slots, factor, got)
    return spectrum_next, tile_spectra


def solution(mesh):
    return jax.shard_map(
        shards,
        mesh=mesh,
        in_specs=(
            P("spec", "space", None),
            P("space", None),
            P("space", None),
            P("space", None),
            P("space", None),
            P("space", None),
            P(),
        ),
        out_specs=(P("spec", "space", None), P(("spec", "space"), None, None)),
        check_vma=False,
    )
```

```python
import math

import jax
import jax.numpy as jnp
import numpy as np
from jax import lax
from jax.experimental import pallas as pl
from jax.experimental.pallas import tpu as pltpu
from jax.sharding import PartitionSpec as P

NDIR = 36
NFREQ = 16
NBINS = NDIR * NFREQ
ROWS = 32
COLS = 512
LANES = 128
LTILES = COLS // LANES
STILES = ROWS // 8
DEVICES = 128
OWN = 8
SLOT = NDIR + 1
QUARTER = NDIR // 4
HALF = NDIR // 2
PLANE = NDIR * ROWS
STEP = ROWS + 1
GROWN = (NDIR * STEP + 7) // 8 * 8
EDGE_ROWS = (0, 1, ROWS - 2, ROWS - 1)
EDGE_PAD = 40
PARTS = 4
FREQ_RATIO = 1.1
COURANT = 0.45

THETA = [2.0 * math.pi * (k + 0.5) / NDIR for k in range(NDIR)]
COS = [float(np.float32(math.cos(t))) for t in THETA]
SIN = [float(np.float32(math.sin(t))) for t in THETA]
ABS_X = [float(np.float32(COURANT * abs(math.cos(t)))) for t in THETA]
ABS_Y = [float(np.float32(COURANT * abs(math.sin(t)))) for t in THETA]
SPEED = np.array([FREQ_RATIO ** (-i) for i in range(NFREQ)], np.float32)
QUADRANTS = ((0, 1, 1), (QUARTER, -1, 1), (2 * QUARTER, -1, -1), (3 * QUARTER, 1, -1))
DOWNWARD = list(range(QUARTER)) + list(range(3 * QUARTER, NDIR))
UPWARD = list(range(QUARTER, 3 * QUARTER))

SMEM_SPEC = pl.BlockSpec(memory_space=pltpu.SMEM)
VMEM_SPEC = pl.BlockSpec(memory_space=pltpu.VMEM)
HBM_SPEC = pl.BlockSpec(memory_space=pltpu.HBM)
PARAMS = pltpu.CompilerParams(vmem_limit_bytes=16 * 1024 * 1024)
F32 = jnp.float32


def speed_of(at_ref):
    index = at_ref[0]
    speed = jnp.float32(1.0)
    for bit in (1, 2, 4, 8):
        speed = speed * jnp.where((index & bit) != 0, jnp.float32(FREQ_RATIO ** (-bit)), jnp.float32(1.0))
    return speed


def in_hbm(x):
    return pltpu.with_memory_space_constraint(x, pltpu.HBM)


def lane_tile(j):
    return pl.ds(j * LANES, LANES)


def iotas():
    return (lax.broadcasted_iota(jnp.int32, (8, LANES), 0), lax.broadcasted_iota(jnp.int32, (8, LANES), 1))


def column_shift(tiles, sign, lane):
    edge = 0 if sign > 0 else LANES - 1
    turned = [pltpu.roll(t, 1 if sign > 0 else LANES - 1, 1) for t in tiles]
    zero = jnp.zeros_like(tiles[0])
    out = []
    for j in range(len(tiles)):
        at = j - sign
        out.append(jnp.where(lane == edge, turned[at] if 0 <= at < len(tiles) else zero, turned[j]))
    return out


def row_shift(tiles, sign, sub):
    edge = 0 if sign > 0 else 7
    turned = [pltpu.roll(t, 1 if sign > 0 else 7, 0) for t in tiles]
    zero = jnp.zeros_like(tiles[0])
    out = []
    for i in range(len(tiles)):
        at = i - sign
        out.append(jnp.where(sub == edge, turned[at] if 0 <= at < len(tiles) else zero, turned[i]))
    return out


def advance(energy, flux, ax, ay, sx, sy, sub, lane):
    n = len(energy)
    by_col = [column_shift(flux[i], sy, lane) for i in range(n)]
    total = ax + ay
    out = [[None] * LTILES for _ in range(n)]
    for j in range(LTILES):
        by_row = row_shift([flux[i][j] for i in range(n)], sx, sub)
        for i in range(n):
            out[i][j] = energy[i][j] - total * flux[i][j] + ax * by_row[i] + ay * by_col[i][j]
    return out


def edge_kernel(at_ref, e_ref, cel_ref, mask_ref, down_ref, up_ref, top_e, bot_e, cels, masks, sems):
    copies = [
        pltpu.make_async_copy(e_ref.at[pl.ds(QUARTER, HALF), pl.ds(0, 8), :], top_e, sems.at[0]),
        pltpu.make_async_copy(e_ref.at[pl.ds(0, QUARTER), pl.ds(ROWS - 8, 8), :], bot_e.at[pl.ds(0, QUARTER)], sems.at[1]),
        pltpu.make_async_copy(
            e_ref.at[pl.ds(3 * QUARTER, QUARTER), pl.ds(ROWS - 8, 8), :], bot_e.at[pl.ds(QUARTER, QUARTER)], sems.at[2]
        ),
        pltpu.make_async_copy(cel_ref.at[pl.ds(0, 8), :], cels.at[0], sems.at[3]),
        pltpu.make_async_copy(cel_ref.at[pl.ds(ROWS - 8, 8), :], cels.at[1], sems.at[4]),
        pltpu.make_async_copy(mask_ref.at[pl.ds(0, 8), :], masks.at[0], sems.at[5]),
        pltpu.make_async_copy(mask_ref.at[pl.ds(ROWS - 8, 8), :], masks.at[1], sems.at[6]),
    ]
    for copy in copies:
        copy.start()
    sub, lane = iotas()
    speed = speed_of(at_ref)
    for copy in copies:
        copy.wait()
    for side, dirs, src, out, row, sx in ((0, UPWARD, top_e, up_ref, 0, -1), (1, DOWNWARD, bot_e, down_ref, 7, 1)):
        cw = [cels[side, :, lane_tile(j)] * masks[side, :, lane_tile(j)].astype(F32) for j in range(LTILES)]
        for i, k in enumerate(dirs):
            ax, ay = speed * ABS_X[k], speed * ABS_Y[k]
            energy = [src[i, :, lane_tile(j)] for j in range(LTILES)]
            flux = [cw[j] * energy[j] for j in range(LTILES)]
            after = advance([energy], [flux], ax, ay, sx, 1 if SIN[k] > 0 else -1, sub, lane)[0]
            for j in range(LTILES):
                out[pl.ds(j * NDIR + i, 1), :] = flux[j][row : row + 1]
                out[pl.ds(j * NDIR + HALF + i, 1), :] = (cw[j] * after[j])[row : row + 1]


def main_kernel(
    at_ref, e_hbm, cel_ref, mask_ref, turn_ref, wind_ref, angle_ref,
    grown_ref, sum_ref, rim_ref, e_ref, e2_ref, cw_ref, table_ref, sems,
):
    copies = []
    for n, (first, _, _) in enumerate(QUADRANTS):
        cut = pl.ds(first, QUARTER)
        copies.append(pltpu.make_async_copy(e_hbm.at[cut], e_ref.at[cut], sems.at[n]))
        copies[-1].start()
    sub, lane = iotas()
    speed = speed_of(at_ref)
    cw_ref[...] = cel_ref[...] * mask_ref[...].astype(F32)
    for k in range(NDIR):
        table_ref[0, k] = speed * ABS_X[k]
        table_ref[1, k] = speed * ABS_Y[k]

    for n, (first, sx, sy) in enumerate(QUADRANTS):
        copies[n].wait()

        def body(i, carry):
            k = first + i
            ax, ay = table_ref[0, k], table_ref[1, k]
            cw = [[cw_ref[pl.ds(8 * r, 8), lane_tile(j)] for j in range(LTILES)] for r in range(STILES)]
            energy = [[e_ref[k, pl.ds(8 * r, 8), lane_tile(j)] for j in range(LTILES)] for r in range(STILES)]
            for _ in range(2):
                flux = [[cw[r][j] * energy[r][j] for j in range(LTILES)] for r in range(STILES)]
                energy = advance(energy, flux, ax, ay, sx, sy, sub, lane)
            for r in range(STILES):
                for j in range(LTILES):
                    e2_ref[j, pl.ds(pl.multiple_of(k * ROWS, 8) + 8 * r, 8), :] = energy[r][j]
            return carry

        lax.fori_loop(0, QUARTER, body, 0, unroll=3)

    def grow(j, carry):
        cols = pl.ds(pl.multiple_of(j * LANES, LANES), LANES)
        wet = mask_ref[:, cols].astype(F32)
        turn = turn_ref[:, cols] * speed
        wind = wind_ref[:, cols]
        angle = angle_ref[:, cols]
        stay = wet * (1.0 - jnp.abs(turn))
        from_low = wet * jnp.maximum(turn, 0.0)
        from_high = wet * jnp.maximum(-turn, 0.0)
        cosine = jnp.cos(angle)
        sine = jnp.sin(angle)
        gain = (0.3 * speed) * wind
        force = wet * 0.05 * wind * wind

        def load(k):
            return e2_ref[j, pl.ds((k % NDIR) * ROWS, ROWS), :]

        low, here = load(NDIR - 1), load(0)
        total = jnp.zeros((ROWS, LANES), F32)
        for k in range(NDIR):
            high = load(k + 1)
            refracted = here * stay + low * from_low + high * from_high
            total = total + refracted
            s = jnp.maximum(cosine * COS[k] + sine * SIN[k], 0.0)
            s = s * s
            grown_ref[j, pl.ds(k * STEP, ROWS), :] = refracted * (1.0 + gain * s) + force * s
            low, here = here, high
        sum_ref[j] = total
        for e, row in enumerate(EDGE_ROWS):
            for b in range(0, NDIR, 8):
                n = min(8, NDIR - b)
                rim_ref[e, j, pl.ds(b, n), :] = e2_ref[j, pl.ds(b * ROWS + row, n, stride=ROWS), :]
        return carry

    lax.fori_loop(0, LTILES, grow, 0)


def rim_kernel(
    at_ref, dirs_ref, grown_in, sum_in, rim_ref, above_ref, below_ref,
    cel_ref, mask_ref, turn_ref, wind_ref, angle_ref,
    grown_ref, sum_ref, ext_ref,
):
    del grown_in
    speed = speed_of(at_ref)
    sum_ref[...] = sum_in[...]
    sub = lax.broadcasted_iota(jnp.int32, (HALF, LANES), 0)
    lane = lax.broadcasted_iota(jnp.int32, (HALF, LANES), 1)
    zero = jnp.zeros((HALF, LANES), F32)
    for side, halo_ref, row in ((0, above_ref, 0), (1, below_ref, ROWS - 1)):
        ax, ay = speed * dirs_ref[2 + 2 * side, 0:HALF, :], speed * dirs_ref[3 + 2 * side, 0:HALF, :]
        first = [ax * halo_ref[pl.ds(j * NDIR, HALF), :] for j in range(LTILES)]
        flux = [
            first[j] * (cel_ref[row : row + 1, lane_tile(j)] * mask_ref[row : row + 1, lane_tile(j)].astype(F32))
            for j in range(LTILES)
        ]
        right = [pltpu.roll(f, 1, 1) for f in flux]
        left = [pltpu.roll(f, LANES - 1, 1) for f in flux]
        for j in range(LTILES):
            r = jnp.where(lane == 0, right[j - 1] if j > 0 else zero, right[j])
            l = jnp.where(lane == LANES - 1, left[j + 1] if j + 1 < LTILES else zero, left[j])
            shifted = jnp.where(sub < QUARTER, r, l)
            outer = first[j] - (ax + ay) * flux[j] + ax * halo_ref[pl.ds(j * NDIR + HALF, HALF), :] + ay * shifted
            inner = ax * flux[j]
            for e, part in ((3 * side, outer), (1 + side, inner)):
                at = EDGE_ROWS[e]
                ext_ref[1 : 1 + NDIR, :] = rim_ref[e, j, 0:NDIR, :]
                if side == 0:
                    ext_ref[1 : 1 + QUARTER, :] += part[:QUARTER]
                    ext_ref[1 + 3 * QUARTER : 1 + NDIR, :] += part[QUARTER:]
                else:
                    ext_ref[1 + QUARTER : 1 + 3 * QUARTER, :] += part
                ext_ref[0:1, :] = ext_ref[NDIR : NDIR + 1, :]
                ext_ref[NDIR + 1 : NDIR + 2, :] = ext_ref[1:2, :]
                cut = (slice(at, at + 1), lane_tile(j))
                wet = mask_ref[cut].astype(F32)
                turn = turn_ref[cut] * speed
                wind = wind_ref[cut]
                angle = angle_ref[cut]
                refracted = (
                    ext_ref[1 : 1 + NDIR, :] * (wet * (1.0 - jnp.abs(turn)))
                    + ext_ref[0:NDIR, :] * (wet * jnp.maximum(turn, 0.0))
                    + ext_ref[2 : 2 + NDIR, :] * (wet * jnp.maximum(-turn, 0.0))
                )
                s = jnp.maximum(dirs_ref[0, 0:NDIR, :] * jnp.cos(angle) + dirs_ref[1, 0:NDIR, :] * jnp.sin(angle), 0.0)
                s = s * s
                grown = refracted * (1.0 + ((0.3 * speed) * wind) * s) + (wet * 0.05 * wind * wind) * s
                for b in range(0, NDIR, 8):
                    n = min(8, NDIR - b)
                    grown_ref[j, pl.ds(b * STEP + at, n, stride=STEP), :] = grown[b : b + n]
                sum_ref[j, at : at + 1, :] = jnp.sum(refracted, axis=0, keepdims=True)


def pack_kernel(picked_ref, grown_ref, sum_ref, out_ref, send_ref, sems):
    copies = []
    for part in range(PARTS):

        def pack(g, carry):
            base = pl.multiple_of(g * (8 * SLOT), 8)
            for d in range(8):
                tile = picked_ref[g * 8 + d]
                row, col = tile >> 2, tile & 3
                at = base + d * SLOT
                for b in range(0, NDIR, 8):
                    n = min(8, NDIR - b)
                    send_ref[pl.ds(at + b, n), :] = grown_ref[col, pl.ds(b * STEP + row, n, stride=STEP), :]
                send_ref[pl.ds(at + NDIR, 1), :] = sum_ref[col, pl.ds(row, 1), :]
            return carry

        groups = DEVICES // 8 // PARTS
        lax.fori_loop(part * groups, (part + 1) * groups, pack, 0)
        cut = pl.ds(part * groups * 8 * SLOT, groups * 8 * SLOT)
        copies.append(pltpu.make_async_copy(send_ref.at[cut], out_ref.at[cut], sems.at[part]))
        copies[-1].start()
    for copy in copies:
        copy.wait()


def home_kernel(at_ref, grown_ref, mine_ref, other_ref, out_ref, stage_ref, scale_ref, sems):
    speed = speed_of(at_ref)
    for j in range(LTILES):
        mean = (mine_ref[j] + other_ref[j]) * (1.0 / NBINS)
        scale_ref[j] = 1.0 / (1.0 + (2.0 * speed * speed) * mean / (1.0 + mean))
    copies = []
    for part in range(4):
        for j in range(LTILES):
            scale = scale_ref[j]
            for k in range(part * QUARTER, (part + 1) * QUARTER):
                stage_ref[k, :, lane_tile(j)] = grown_ref[j, pl.ds(k * STEP, ROWS), :] * scale
        cut = pl.ds(part * QUARTER, QUARTER)
        copies.append(pltpu.make_async_copy(stage_ref.at[cut], out_ref.at[cut], sems.at[part]))
        copies[-1].start()
    for copy in copies:
        copy.wait()


def owner_kernel(slots_ref, factor_ref, got_ref, out_ref, stage_ref, scale_ref, sems):
    copies = []
    for b in range(OWN):
        sums = got_ref[pl.ds(b * SLOT + NDIR, NFREQ, stride=OWN * SLOT), :]
        mean = jnp.sum(sums, axis=0, keepdims=True) * (1.0 / NBINS)
        scale_ref[b] = 1.0 / (1.0 + factor_ref[...] * mean / (1.0 + mean))
    for b in range(OWN):
        for s in range(NFREQ):
            stage_ref[b, pl.ds(s * NDIR, NDIR), :] = (
                got_ref[pl.ds((s * OWN + b) * SLOT, NDIR), :] * scale_ref[b, s : s + 1, :]
            )
        copies.append(pltpu.make_async_copy(stage_ref.at[b], out_ref.at[slots_ref[b]], sems.at[b]))
        copies[-1].start()
    for copy in copies:
        copy.wait()


def shards(spectrum, land_mask, celerity, turning, wind_speed, wind_dir, tile_order):
    band = lax.axis_index("space")
    me = lax.axis_index(("spec", "space"))
    at = lax.axis_index("spec").astype(jnp.int32).reshape(1)
    space_count = lax.axis_size("space")
    spec_count = lax.axis_size("spec")
    shape = jax.ShapeDtypeStruct

    down, up = pl.pallas_call(
        edge_kernel,
        out_shape=(shape((LTILES * NDIR, LANES), F32),) * 2,
        in_specs=[SMEM_SPEC] + [HBM_SPEC] * 3,
        out_specs=(VMEM_SPEC,) * 2,
        scratch_shapes=[
            pltpu.VMEM((HALF, 8, COLS), F32),
            pltpu.VMEM((HALF, 8, COLS), F32),
            pltpu.VMEM((2, 8, COLS), F32),
            pltpu.VMEM((2, 8, COLS), jnp.int32),
            pltpu.SemaphoreType.DMA((7,)),
        ],
        compiler_params=PARAMS,
        name="edges",
    )(at, in_hbm(spectrum), in_hbm(celerity), in_hbm(land_mask))
    above = lax.ppermute(down, "space", [(i, i + 1) for i in range(space_count - 1)])
    below = lax.ppermute(up, "space", [(i + 1, i) for i in range(space_count - 1)])

    per_band = ROWS * LTILES
    order = tile_order.reshape(DEVICES, OWN)
    picked = jnp.sum(jnp.where(order // per_band == band, order % per_band, 0), axis=1).astype(jnp.int32)
    own = lax.dynamic_slice_in_dim(order, me, 1, 0).reshape(OWN) // per_band
    slots = jnp.sum(
        jnp.where(own[None, :] == jnp.arange(OWN)[:, None], jnp.arange(OWN)[None, :], 0), axis=1
    ).astype(jnp.int32)

    grown, sums, rim = pl.pallas_call(
        main_kernel,
        out_shape=(
            shape((LTILES, GROWN, LANES), F32),
            shape((LTILES, ROWS, LANES), F32),
            shape((len(EDGE_ROWS), LTILES, EDGE_PAD, LANES), F32),
        ),
        in_specs=[SMEM_SPEC, HBM_SPEC] + [VMEM_SPEC] * 5,
        out_specs=(VMEM_SPEC,) * 3,
        scratch_shapes=[
            pltpu.VMEM((NDIR, ROWS, COLS), F32),
            pltpu.VMEM((LTILES, PLANE, LANES), F32),
            pltpu.VMEM((ROWS, COLS), F32),
            pltpu.SMEM((2, NDIR), F32),
            pltpu.SemaphoreType.DMA((4,)),
        ],
        compiler_params=PARAMS,
        name="bins",
    )(at, in_hbm(spectrum), celerity, land_mask, turning, wind_speed, wind_dir)

    table = np.zeros((6, EDGE_PAD, LANES), np.float32)
    for i, row in enumerate((COS, SIN)):
        table[i, :NDIR] = np.array(row, np.float32)[:, None]
    for i, dirs in enumerate((DOWNWARD, UPWARD)):
        table[2 + 2 * i, :HALF] = np.array([ABS_X[k] for k in dirs], np.float32)[:, None]
        table[3 + 2 * i, :HALF] = np.array([ABS_Y[k] for k in dirs], np.float32)[:, None]
    grown, sums = pl.pallas_call(
        rim_kernel,
        out_shape=(
            shape((LTILES, GROWN, LANES), F32),
            shape((LTILES, ROWS, LANES), F32),
        ),
        in_specs=[SMEM_SPEC] + [VMEM_SPEC] * 11,
        out_specs=(VMEM_SPEC,) * 2,
        scratch_shapes=[pltpu.VMEM((EDGE_PAD, LANES), F32)],
        input_output_aliases={2: 0},
        compiler_params=PARAMS,
        name="rims",
    )(at, jnp.asarray(table), grown, sums, rim, above, below, celerity, land_mask, turning, wind_speed, wind_dir)

    send = pl.pallas_call(
        pack_kernel,
        out_shape=pltpu.HBM((DEVICES * SLOT, LANES), F32),
        in_specs=[SMEM_SPEC] + [VMEM_SPEC] * 2,
        out_specs=HBM_SPEC,
        scratch_shapes=[pltpu.VMEM((DEVICES * SLOT, LANES), F32), pltpu.SemaphoreType.DMA((PARTS,))],
        compiler_params=PARAMS,
        name="pack",
    )(picked, grown, sums)

    pair = lax.ppermute(sums, "spec", [(i, i ^ 1) for i in range(spec_count)])
    send, pair = lax.optimization_barrier((send, pair))
    pairs = sums + pair
    got = lax.all_to_all(
        send.reshape(DEVICES, SLOT, 1, LANES), ("spec", "space"), split_axis=0, concat_axis=0, tiled=True
    ).reshape(DEVICES * SLOT, LANES)
    parts = [lax.ppermute(pairs, "spec", [(i, i ^ (4 * n)) for i in range(spec_count)]) for n in range(1, 4)]
    eights = pairs + parts[0] + parts[1] + parts[2]
    other = lax.ppermute(eights, "spec", [(i, i ^ 2) for i in range(spec_count)])

    factor = jnp.asarray(np.repeat(2.0 * SPEED[:, None] * SPEED[:, None], LANES, axis=1), F32)
    tile_spectra = pl.pallas_call(
        owner_kernel,
        out_shape=shape((OWN, NBINS, LANES), F32),
        in_specs=[SMEM_SPEC] + [VMEM_SPEC] * 2,
        out_specs=HBM_SPEC,
        scratch_shapes=[
            pltpu.VMEM((OWN, NBINS, LANES), F32),
            pltpu.VMEM((OWN, NFREQ, LANES), F32),
            pltpu.SemaphoreType.DMA((OWN,)),
        ],
        compiler_params=PARAMS,
        name="owned",
    )(slots, factor, got)

    other, tile_spectra = lax.optimization_barrier((other, tile_spectra))
    spectrum_next = pl.pallas_call(
        home_kernel,
        out_shape=shape((NDIR, ROWS, COLS), F32),
        in_specs=[SMEM_SPEC] + [VMEM_SPEC] * 3,
        out_specs=HBM_SPEC,
        scratch_shapes=[
            pltpu.VMEM((NDIR, ROWS, COLS), F32),
            pltpu.VMEM((LTILES, ROWS, LANES), F32),
            pltpu.SemaphoreType.DMA((4,)),
        ],
        compiler_params=PARAMS,
        name="home",
    )(at, grown, eights, other)
    return spectrum_next, tile_spectra


def solution(mesh):
    return jax.shard_map(
        shards,
        mesh=mesh,
        in_specs=(
            P("spec", "space", None),
            P("space", None),
            P("space", None),
            P("space", None),
            P("space", None),
            P("space", None),
            P(),
        ),
        out_specs=(P("spec", "space", None), P(("spec", "space"), None, None)),
        check_vma=False,
    )
```

```python
import math

import jax
import jax.numpy as jnp
import numpy as np
from jax import lax
from jax.experimental import pallas as pl
from jax.experimental.pallas import tpu as pltpu
from jax.sharding import PartitionSpec as P

NDIR = 36
NFREQ = 16
NBINS = NDIR * NFREQ
ROWS = 32
COLS = 512
LANES = 128
LTILES = COLS // LANES
STILES = ROWS // 8
DEVICES = 128
OWN = 8
SLOT = NDIR + 1
QUARTER = NDIR // 4
HALF = NDIR // 2
STEP = ROWS + 1
GROWN = (NDIR * STEP + 7) // 8 * 8
EDGE_PAD = 24
PIECE = 3
FREQ_RATIO = 1.1
COURANT = 0.45

THETA = [2.0 * math.pi * (k + 0.5) / NDIR for k in range(NDIR)]
COS = [float(np.float32(math.cos(t))) for t in THETA]
SIN = [float(np.float32(math.sin(t))) for t in THETA]
ABS_X = [float(np.float32(COURANT * abs(math.cos(t)))) for t in THETA]
ABS_Y = [float(np.float32(COURANT * abs(math.sin(t)))) for t in THETA]
SPEED = np.array([FREQ_RATIO ** (-i) for i in range(NFREQ)], np.float32)
DOWNWARD = list(range(QUARTER)) + list(range(3 * QUARTER, NDIR))
UPWARD = list(range(QUARTER, 3 * QUARTER))

SMEM_SPEC = pl.BlockSpec(memory_space=pltpu.SMEM)
VMEM_SPEC = pl.BlockSpec(memory_space=pltpu.VMEM)
HBM_SPEC = pl.BlockSpec(memory_space=pltpu.HBM)
ANY_SPEC = pl.BlockSpec(memory_space=pl.ANY)
PARAMS = pltpu.CompilerParams(vmem_limit_bytes=16 * 1024 * 1024)
F32 = jnp.float32


def speed_of(at_ref):
    index = at_ref[0] >> 3
    speed = jnp.float32(1.0)
    for bit in (1, 2, 4, 8):
        speed = speed * jnp.where((index & bit) != 0, jnp.float32(FREQ_RATIO ** (-bit)), jnp.float32(1.0))
    return speed


def in_hbm(x):
    return pltpu.with_memory_space_constraint(x, pltpu.HBM)


def lane_tile(j):
    return pl.ds(j * LANES, LANES)


def iotas():
    return (lax.broadcasted_iota(jnp.int32, (8, LANES), 0), lax.broadcasted_iota(jnp.int32, (8, LANES), 1))


def column_shift(tiles, sign, lane):
    edge = 0 if sign > 0 else LANES - 1
    turned = [pltpu.roll(t, 1 if sign > 0 else LANES - 1, 1) for t in tiles]
    zero = jnp.zeros_like(tiles[0])
    out = []
    for j in range(len(tiles)):
        at = j - sign
        out.append(jnp.where(lane == edge, turned[at] if 0 <= at < len(tiles) else zero, turned[j]))
    return out


def row_shift(tiles, sign, sub):
    edge = 0 if sign > 0 else 7
    turned = [pltpu.roll(t, 1 if sign > 0 else 7, 0) for t in tiles]
    zero = jnp.zeros_like(tiles[0])
    out = []
    for i in range(len(tiles)):
        at = i - sign
        out.append(jnp.where(sub == edge, turned[at] if 0 <= at < len(tiles) else zero, turned[i]))
    return out


def advance(energy, flux, ax, ay, sx, sy, sub, lane):
    n = len(energy)
    by_col = [column_shift(flux[i], sy, lane) for i in range(n)]
    total = ax + ay
    out = [[None] * LTILES for _ in range(n)]
    for j in range(LTILES):
        by_row = row_shift([flux[i][j] for i in range(n)], sx, sub)
        for i in range(n):
            out[i][j] = energy[i][j] - total * flux[i][j] + ax * by_row[i] + ay * by_col[i][j]
    return out


def edge_kernel(at_ref, e_ref, cel_ref, mask_ref, near_ref, far_ref, up_e_ref, edge_e, cels, masks, rim_ref, sems):
    copies = [
        pltpu.make_async_copy(e_ref.at[pl.ds(0, QUARTER), pl.ds(ROWS - 8, 8), :], edge_e.at[0, pl.ds(0, QUARTER)], sems.at[0]),
        pltpu.make_async_copy(
            e_ref.at[pl.ds(3 * QUARTER, QUARTER), pl.ds(ROWS - 8, 8), :], edge_e.at[0, pl.ds(QUARTER, QUARTER)], sems.at[1]
        ),
        pltpu.make_async_copy(e_ref.at[pl.ds(QUARTER, HALF), pl.ds(0, 8), :], edge_e.at[1], sems.at[2]),
        pltpu.make_async_copy(cel_ref.at[pl.ds(ROWS - 8, 8), :], cels.at[0], sems.at[3]),
        pltpu.make_async_copy(mask_ref.at[pl.ds(ROWS - 8, 8), :], masks.at[0], sems.at[4]),
        pltpu.make_async_copy(cel_ref.at[pl.ds(0, 8), :], cels.at[1], sems.at[5]),
        pltpu.make_async_copy(mask_ref.at[pl.ds(0, 8), :], masks.at[1], sems.at[6]),
    ]
    for copy in copies:
        copy.start()
    ahead = pltpu.make_async_copy(e_ref.at[pl.ds(QUARTER, HALF)], up_e_ref, sems.at[7])
    ahead.start()
    sub, lane = iotas()
    speed = speed_of(at_ref)
    odd = at_ref[0] & 1
    for copy in copies:
        copy.wait()
    for side, dirs, row, sx in ((0, DOWNWARD, 7, 1), (1, UPWARD, 0, -1)):
        cw = [cels[side, :, lane_tile(j)] * masks[side, :, lane_tile(j)].astype(F32) for j in range(LTILES)]
        out = odd if side == 0 else 1 - odd
        for i, k in enumerate(dirs):
            ax, ay = speed * ABS_X[k], speed * ABS_Y[k]
            energy = [edge_e[side, i, :, lane_tile(j)] for j in range(LTILES)]
            flux = [cw[j] * energy[j] for j in range(LTILES)]
            after = advance([energy], [flux], ax, ay, sx, 1 if SIN[k] > 0 else -1, sub, lane)[0]
            for j in range(LTILES):
                rim_ref[out, pl.ds(j * NDIR + i, 1), :] = flux[j][row : row + 1]
                rim_ref[out, pl.ds(j * NDIR + HALF + i, 1), :] = (cw[j] * after[j])[row : row + 1]
    near_ref[...] = rim_ref[0]
    far_ref[...] = rim_ref[1]
    ahead.wait()


def propagate(speed, dirs, sx, e_ref, cw_ref, table_ref, e2_ref, sum_ref):
    sub, lane = iotas()
    for i, k in enumerate(dirs):
        table_ref[0, i] = speed * ABS_X[k]
        table_ref[1, i] = speed * ABS_Y[k]

    for half, sy in ((0, 1), (1, -1)):

        def body(piece, carry):
            total = None
            for d in range(PIECE):
                i = half * QUARTER + piece * PIECE + d
                ax, ay = table_ref[0, i], table_ref[1, i]
                cw = [[cw_ref[pl.ds(8 * r, 8), lane_tile(j)] for j in range(LTILES)] for r in range(STILES)]
                energy = [[e_ref[i, pl.ds(8 * r, 8), lane_tile(j)] for j in range(LTILES)] for r in range(STILES)]
                for _ in range(2):
                    flux = [[cw[r][j] * energy[r][j] for j in range(LTILES)] for r in range(STILES)]
                    energy = advance(energy, flux, ax, ay, sx, sy, sub, lane)
                for r in range(STILES):
                    for j in range(LTILES):
                        e2_ref[j, pl.ds(pl.multiple_of(i * ROWS, 8) + 8 * r, 8), :] = energy[r][j]
                total = energy if total is None else [[t + e for t, e in zip(x, y)] for x, y in zip(total, energy)]
            for r in range(STILES):
                for j in range(LTILES):
                    sum_ref[j, pl.ds(8 * r, 8), :] += total[r][j]
            return carry

        lax.fori_loop(0, QUARTER // PIECE, body, 0)


def upward_kernel(
    at_ref, e_hbm, e_ref, cel_ref, mask_ref, pass_in, e2_ref, sum_ref, pass_ref, down_e_ref, cw_ref, table_ref, sems
):
    ahead = [
        pltpu.make_async_copy(e_hbm.at[pl.ds(0, QUARTER)], down_e_ref.at[pl.ds(0, QUARTER)], sems.at[0]),
        pltpu.make_async_copy(e_hbm.at[pl.ds(3 * QUARTER, QUARTER)], down_e_ref.at[pl.ds(QUARTER, QUARTER)], sems.at[1]),
    ]
    for copy in ahead:
        copy.start()
    cw_ref[...] = cel_ref[...] * mask_ref[...].astype(F32)
    sum_ref[...] = jnp.zeros_like(sum_ref)
    pass_ref[...] = pass_in[...]
    propagate(speed_of(at_ref), UPWARD, -1, e_ref, cw_ref, table_ref, e2_ref, sum_ref)
    for copy in ahead:
        copy.wait()


def downward_kernel(at_ref, e_ref, cel_ref, mask_ref, sum_in, e2_ref, sum_ref, cw_ref, table_ref):
    cw_ref[...] = cel_ref[...] * mask_ref[...].astype(F32)
    sum_ref[...] = sum_in[...]
    propagate(speed_of(at_ref), DOWNWARD, 1, e_ref, cw_ref, table_ref, e2_ref, sum_ref)


def rim_kernel(
    at_ref, dirs_ref, up_in, down_in, sum_in, near_ref, far_ref, cel_ref, mask_ref,
    up_ref, down_ref, sum_ref, halos_ref,
):
    del up_in, down_in
    speed = speed_of(at_ref)
    odd = at_ref[0] & 1
    halos_ref[1 - odd] = near_ref[...]
    halos_ref[odd] = far_ref[...]
    for j in range(LTILES):
        sum_ref[j] = sum_in[j] * mask_ref[:, lane_tile(j)].astype(F32)
    sub = lax.broadcasted_iota(jnp.int32, (HALF, LANES), 0)
    lane = lax.broadcasted_iota(jnp.int32, (HALF, LANES), 1)
    zero = jnp.zeros((HALF, LANES), F32)
    for side, e2_ref, row, inside in ((0, down_ref, 0, 1), (1, up_ref, ROWS - 1, ROWS - 2)):
        ax, ay = speed * dirs_ref[2 * side, 0:HALF, :], speed * dirs_ref[2 * side + 1, 0:HALF, :]
        first = [ax * halos_ref[side, pl.ds(j * NDIR, HALF), :] for j in range(LTILES)]
        flux = [
            first[j] * (cel_ref[row : row + 1, lane_tile(j)] * mask_ref[row : row + 1, lane_tile(j)].astype(F32))
            for j in range(LTILES)
        ]
        right = [pltpu.roll(f, 1, 1) for f in flux]
        left = [pltpu.roll(f, LANES - 1, 1) for f in flux]
        for j in range(LTILES):
            r = jnp.where(lane == 0, right[j - 1] if j > 0 else zero, right[j])
            l = jnp.where(lane == LANES - 1, left[j + 1] if j + 1 < LTILES else zero, left[j])
            shifted = jnp.where(sub < QUARTER, r, l)
            outer = first[j] - (ax + ay) * flux[j] + ax * halos_ref[side, pl.ds(j * NDIR + HALF, HALF), :] + ay * shifted
            inner = ax * flux[j]
            for at, part in ((row, outer), (inside, inner)):
                for b in range(0, HALF, 8):
                    n = min(8, HALF - b)
                    cut = pl.ds(b * ROWS + at, n, stride=ROWS)
                    e2_ref[j, cut, :] = e2_ref[j, cut, :] + part[b : b + n]
                wet = mask_ref[at : at + 1, lane_tile(j)].astype(F32)
                sum_ref[j, at : at + 1, :] += wet * jnp.sum(part, axis=0, keepdims=True)


def grow_kernel(
    at_ref, picked_hbm, up_ref, down_ref, sum_ref, mask_ref, turn_ref, wind_ref, angle_ref,
    grown_hbm, out_ref, grown_ref, send_ref, picked_ref, to_ref, sems,
):
    fetch = pltpu.make_async_copy(picked_hbm, picked_ref, sems.at[LTILES + 1])
    fetch.start()

    def invert(g, carry):
        for d in range(8):
            to_ref[picked_ref[g * 8 + d]] = g * 8 + d
        return carry

    rows_ref = send_ref.reshape(DEVICES * SLOT, LANES)
    speed = speed_of(at_ref)

    def grow(j, carry):
        cols = pl.ds(pl.multiple_of(j * LANES, LANES), LANES)
        wet = mask_ref[:, cols].astype(F32)
        turn = turn_ref[:, cols] * speed
        wind = wind_ref[:, cols]
        angle = angle_ref[:, cols]
        stay = wet * (1.0 - jnp.abs(turn))
        from_low = wet * jnp.maximum(turn, 0.0)
        from_high = wet * jnp.maximum(-turn, 0.0)
        cosine = jnp.cos(angle)
        sine = jnp.sin(angle)
        gain = (0.3 * speed) * wind
        force = wet * 0.05 * wind * wind

        def load(k):
            k = k % NDIR
            ref, i = (up_ref, k - QUARTER) if k in UPWARD else (down_ref, DOWNWARD.index(k))
            return ref[j, pl.ds(i * ROWS, ROWS), :]

        low, here = load(NDIR - 1), load(0)
        for k in range(NDIR):
            high = load(k + 1)
            refracted = here * stay + low * from_low + high * from_high
            s = jnp.maximum(cosine * COS[k] + sine * SIN[k], 0.0)
            s = s * s
            grown_ref[j, pl.ds(k * STEP, ROWS), :] = refracted * (1.0 + gain * s) + force * s
            low, here = here, high
        pltpu.make_async_copy(grown_ref.at[j], grown_hbm.at[j], sems.at[j]).start()

        @pl.when(j == 0)
        def _():
            fetch.wait()
            lax.fori_loop(0, DEVICES // 8, invert, 0)

        def pack(g, carry):
            for r in range(8):
                row = g * 8 + r
                at = (j * ROWS + row) * SLOT
                for b in range(0, NDIR, 8):
                    n = min(8, NDIR - b)
                    rows_ref[pl.ds(at + b, n), :] = grown_ref[j, pl.ds(b * STEP + row, n, stride=STEP), :]
                rows_ref[pl.ds(at + NDIR, 1), :] = sum_ref[j, pl.ds(row, 1), :]
                to = to_ref[row * LTILES + j] * SLOT
                pltpu.make_async_copy(send_ref.at[pl.ds(at, SLOT)], out_ref.at[pl.ds(to, SLOT)], sems.at[LTILES]).start()
            return carry

        lax.fori_loop(0, ROWS // 8, pack, 0)
        return carry

    lax.fori_loop(0, LTILES, grow, 0)
    for j in range(LTILES):
        pltpu.make_async_copy(grown_ref.at[j], grown_hbm.at[j], sems.at[j]).wait()
    pltpu.make_async_copy(send_ref, out_ref, sems.at[LTILES]).wait()


def home_kernel(at_ref, grown_ref, mine_ref, other_ref, out_ref, stage_ref, scale_ref, sems):
    speed = speed_of(at_ref)
    for j in range(LTILES):
        mean = (mine_ref[j] + other_ref[j]) * (1.0 / NBINS)
        scale_ref[j] = 1.0 / (1.0 + (2.0 * speed * speed) * mean / (1.0 + mean))
    copies = []
    for part in range(4):
        for j in range(LTILES):
            scale = scale_ref[j]
            for k in range(part * QUARTER, (part + 1) * QUARTER):
                stage_ref[k, :, lane_tile(j)] = grown_ref[j, pl.ds(k * STEP, ROWS), :] * scale
        cut = pl.ds(part * QUARTER, QUARTER)
        copies.append(pltpu.make_async_copy(stage_ref.at[cut], out_ref.at[cut], sems.at[part]))
        copies[-1].start()
    for copy in copies:
        copy.wait()


def owner_kernel(slots_ref, factor_ref, got_ref, out_ref, stage_ref, scale_ref, sems):
    copies = []
    for b in range(OWN):
        sums = got_ref[pl.ds(b * SLOT + NDIR, NFREQ, stride=OWN * SLOT), :]
        mean = jnp.sum(sums, axis=0, keepdims=True) * (1.0 / NBINS)
        scale_ref[b] = 1.0 / (1.0 + factor_ref[...] * mean / (1.0 + mean))
    for b in range(OWN):
        for s in range(NFREQ):
            stage_ref[b, pl.ds(s * NDIR, NDIR), :] = (
                got_ref[pl.ds((s * OWN + b) * SLOT, NDIR), :] * scale_ref[b, s : s + 1, :]
            )
        copies.append(pltpu.make_async_copy(stage_ref.at[b], out_ref.at[slots_ref[b]], sems.at[b]))
        copies[-1].start()
    for copy in copies:
        copy.wait()


def shards(spectrum, land_mask, celerity, turning, wind_speed, wind_dir, tile_order):
    band = lax.axis_index("space")
    me = lax.axis_index(("spec", "space"))
    at = me.astype(jnp.int32).reshape(1)
    space_count = lax.axis_size("space")
    spec_count = lax.axis_size("spec")
    shape = jax.ShapeDtypeStruct

    planes = shape((HALF, ROWS, COLS), F32)
    halves = shape((LTILES, HALF * ROWS, LANES), F32)
    rims = shape((LTILES * NDIR, LANES), F32)
    summed = shape((LTILES, ROWS, LANES), F32)
    near_rim, far_rim, up_e = pl.pallas_call(
        edge_kernel,
        out_shape=(rims, rims, planes),
        in_specs=[SMEM_SPEC] + [HBM_SPEC] * 3,
        out_specs=(VMEM_SPEC,) * 3,
        scratch_shapes=[
            pltpu.VMEM((2, HALF, 8, COLS), F32),
            pltpu.VMEM((2, 8, COLS), F32),
            pltpu.VMEM((2, 8, COLS), jnp.int32),
            pltpu.VMEM((2, LTILES * NDIR, LANES), F32),
            pltpu.SemaphoreType.DMA((8,)),
        ],
        compiler_params=PARAMS,
        name="edges",
    )(at, in_hbm(spectrum), in_hbm(celerity), in_hbm(land_mask))
    within = [(i, i ^ 1) for i in range(space_count)]
    across = [(i, i + 1) for i in range(1, space_count - 1, 2)]
    across = across + [(b, a) for a, b in across]
    far = lax.ppermute(far_rim, "space", across)
    scratch = [pltpu.VMEM((ROWS, COLS), F32), pltpu.SMEM((2, HALF), F32)]
    up_e2, sums, near_rim, down_e = pl.pallas_call(
        upward_kernel,
        out_shape=(halves, summed, rims, planes),
        in_specs=[SMEM_SPEC, HBM_SPEC] + [VMEM_SPEC] * 4,
        out_specs=(VMEM_SPEC,) * 4,
        scratch_shapes=scratch + [pltpu.SemaphoreType.DMA((2,))],
        compiler_params=PARAMS,
        name="upward",
    )(at, in_hbm(spectrum), up_e, celerity, land_mask, near_rim)
    near = lax.ppermute(near_rim, "space", within)
    down_e2, sums = pl.pallas_call(
        downward_kernel,
        out_shape=(halves, summed),
        in_specs=[SMEM_SPEC] + [VMEM_SPEC] * 4,
        out_specs=(VMEM_SPEC,) * 2,
        scratch_shapes=scratch,
        compiler_params=PARAMS,
        name="downward",
    )(at, down_e, celerity, land_mask, sums)

    per_band = ROWS * LTILES
    order = tile_order.reshape(DEVICES, OWN)
    picked = jnp.sum(jnp.where(order // per_band == band, order % per_band, 0), axis=1).astype(jnp.int32)
    own = lax.dynamic_slice_in_dim(order, me, 1, 0).reshape(OWN) // per_band
    slots = jnp.sum(
        jnp.where(own[None, :] == jnp.arange(OWN)[:, None], jnp.arange(OWN)[None, :], 0), axis=1
    ).astype(jnp.int32)

    table = np.zeros((4, EDGE_PAD, LANES), np.float32)
    for i, dirs in enumerate((DOWNWARD, UPWARD)):
        table[2 * i, :HALF] = np.array([ABS_X[k] for k in dirs], np.float32)[:, None]
        table[2 * i + 1, :HALF] = np.array([ABS_Y[k] for k in dirs], np.float32)[:, None]
    up_e2, down_e2, sums = pl.pallas_call(
        rim_kernel,
        out_shape=(halves, halves, summed),
        in_specs=[SMEM_SPEC] + [VMEM_SPEC] * 8,
        out_specs=(VMEM_SPEC,) * 3,
        scratch_shapes=[pltpu.VMEM((2, LTILES * NDIR, LANES), F32)],
        input_output_aliases={2: 0, 3: 1},
        compiler_params=PARAMS,
        name="rims",
    )(at, jnp.asarray(table), up_e2, down_e2, sums, near, far, celerity, land_mask)

    grown, send = pl.pallas_call(
        grow_kernel,
        out_shape=(pltpu.HBM((LTILES, GROWN, LANES), F32), pltpu.HBM((DEVICES * SLOT, 1, LANES), F32)),
        in_specs=[SMEM_SPEC, ANY_SPEC] + [VMEM_SPEC] * 7,
        out_specs=(HBM_SPEC,) * 2,
        scratch_shapes=[
            pltpu.VMEM((LTILES, GROWN, LANES), F32),
            pltpu.VMEM((DEVICES * SLOT, 1, LANES), F32),
            pltpu.SMEM((DEVICES,), jnp.int32),
            pltpu.SMEM((DEVICES,), jnp.int32),
            pltpu.SemaphoreType.DMA((LTILES + 2,)),
        ],
        compiler_params=PARAMS,
        name="grow",
    )(at, picked, up_e2, down_e2, sums, land_mask, turning, wind_speed, wind_dir)

    pair = lax.ppermute(sums, "spec", [(i, i ^ 1) for i in range(spec_count)])
    send, pair = lax.optimization_barrier((send, pair))
    pairs = sums + pair
    got = lax.all_to_all(
        send.reshape(DEVICES, SLOT, 1, LANES), ("spec", "space"), split_axis=0, concat_axis=0, tiled=True
    ).reshape(DEVICES * SLOT, LANES)
    parts = [lax.ppermute(pairs, "spec", [(i, i ^ n) for i in range(spec_count)]) for n in (3, 4, 7)]
    eights = pairs + parts[0] + parts[1] + parts[2]
    other = lax.ppermute(eights, "spec", [(i, i ^ 8) for i in range(spec_count)])

    factor = jnp.asarray(np.repeat(2.0 * SPEED[:, None] * SPEED[:, None], LANES, axis=1), F32)
    tile_spectra = pl.pallas_call(
        owner_kernel,
        out_shape=shape((OWN, NBINS, LANES), F32),
        in_specs=[SMEM_SPEC] + [VMEM_SPEC] * 2,
        out_specs=HBM_SPEC,
        scratch_shapes=[
            pltpu.VMEM((OWN, NBINS, LANES), F32),
            pltpu.VMEM((OWN, NFREQ, LANES), F32),
            pltpu.SemaphoreType.DMA((OWN,)),
        ],
        compiler_params=PARAMS,
        name="owned",
    )(slots, factor, got)

    other, tile_spectra = lax.optimization_barrier((other, tile_spectra))
    spectrum_next = pl.pallas_call(
        home_kernel,
        out_shape=shape((NDIR, ROWS, COLS), F32),
        in_specs=[SMEM_SPEC] + [VMEM_SPEC] * 3,
        out_specs=HBM_SPEC,
        scratch_shapes=[
            pltpu.VMEM((NDIR, ROWS, COLS), F32),
            pltpu.VMEM((LTILES, ROWS, LANES), F32),
            pltpu.SemaphoreType.DMA((4,)),
        ],
        compiler_params=PARAMS,
        name="home",
    )(at, grown, eights, other)
    return spectrum_next, tile_spectra


def solution(mesh):
    return jax.shard_map(
        shards,
        mesh=mesh,
        in_specs=(
            P("spec", "space", None),
            P("space", None),
            P("space", None),
            P("space", None),
            P("space", None),
            P("space", None),
            P(),
        ),
        out_specs=(P("spec", "space", None), P(("spec", "space"), None, None)),
        check_vma=False,
    )
```

```python
import math

import jax
import jax.numpy as jnp
import numpy as np
from jax import lax
from jax.experimental import pallas as pl
from jax.experimental.pallas import tpu as pltpu
from jax.sharding import PartitionSpec as P

NDIR = 36
NFREQ = 16
NBINS = NDIR * NFREQ
ROWS = 32
COLS = 512
LANES = 128
LTILES = COLS // LANES
STILES = ROWS // 8
DEVICES = 128
OWN = 8
SLOT = NDIR + 1
QUARTER = NDIR // 4
HALF = NDIR // 2
STEP = ROWS + 1
GROWN = (NDIR * STEP + 7) // 8 * 8
EDGE_PAD = 24
PIECE = 3
FREQ_RATIO = 1.1
COURANT = 0.45

THETA = [2.0 * math.pi * (k + 0.5) / NDIR for k in range(NDIR)]
COS = [float(np.float32(math.cos(t))) for t in THETA]
SIN = [float(np.float32(math.sin(t))) for t in THETA]
ABS_X = [float(np.float32(COURANT * abs(math.cos(t)))) for t in THETA]
ABS_Y = [float(np.float32(COURANT * abs(math.sin(t)))) for t in THETA]
SPEED = np.array([FREQ_RATIO ** (-i) for i in range(NFREQ)], np.float32)
DOWNWARD = list(range(QUARTER)) + list(range(3 * QUARTER, NDIR))
UPWARD = list(range(QUARTER, 3 * QUARTER))

SMEM_SPEC = pl.BlockSpec(memory_space=pltpu.SMEM)
VMEM_SPEC = pl.BlockSpec(memory_space=pltpu.VMEM)
HBM_SPEC = pl.BlockSpec(memory_space=pltpu.HBM)
ANY_SPEC = pl.BlockSpec(memory_space=pl.ANY)
PARAMS = pltpu.CompilerParams(vmem_limit_bytes=16 * 1024 * 1024)
F32 = jnp.float32


def speed_of(at_ref):
    index = at_ref[0] >> 3
    speed = jnp.float32(1.0)
    for bit in (1, 2, 4, 8):
        speed = speed * jnp.where((index & bit) != 0, jnp.float32(FREQ_RATIO ** (-bit)), jnp.float32(1.0))
    return speed


def in_hbm(x):
    return pltpu.with_memory_space_constraint(x, pltpu.HBM)


def lane_tile(j):
    return pl.ds(j * LANES, LANES)


def iotas():
    return (lax.broadcasted_iota(jnp.int32, (8, LANES), 0), lax.broadcasted_iota(jnp.int32, (8, LANES), 1))


def column_shift(tiles, sign, lane):
    edge = 0 if sign > 0 else LANES - 1
    turned = [pltpu.roll(t, 1 if sign > 0 else LANES - 1, 1) for t in tiles]
    zero = jnp.zeros_like(tiles[0])
    out = []
    for j in range(len(tiles)):
        at = j - sign
        out.append(jnp.where(lane == edge, turned[at] if 0 <= at < len(tiles) else zero, turned[j]))
    return out


def row_shift(tiles, sign, sub):
    edge = 0 if sign > 0 else 7
    turned = [pltpu.roll(t, 1 if sign > 0 else 7, 0) for t in tiles]
    zero = jnp.zeros_like(tiles[0])
    out = []
    for i in range(len(tiles)):
        at = i - sign
        out.append(jnp.where(sub == edge, turned[at] if 0 <= at < len(tiles) else zero, turned[i]))
    return out


def advance(energy, flux, ax, ay, sx, sy, sub, lane):
    n = len(energy)
    by_col = [column_shift(flux[i], sy, lane) for i in range(n)]
    total = ax + ay
    out = [[None] * LTILES for _ in range(n)]
    for j in range(LTILES):
        by_row = row_shift([flux[i][j] for i in range(n)], sx, sub)
        for i in range(n):
            out[i][j] = energy[i][j] - total * flux[i][j] + ax * by_row[i] + ay * by_col[i][j]
    return out


def edge_kernel(at_ref, e_ref, cel_ref, mask_ref, near_ref, far_ref, up_e_ref, edge_e, cels, masks, rim_ref, sems):
    copies = [
        pltpu.make_async_copy(e_ref.at[pl.ds(0, QUARTER), pl.ds(ROWS - 8, 8), :], edge_e.at[0, pl.ds(0, QUARTER)], sems.at[0]),
        pltpu.make_async_copy(
            e_ref.at[pl.ds(3 * QUARTER, QUARTER), pl.ds(ROWS - 8, 8), :], edge_e.at[0, pl.ds(QUARTER, QUARTER)], sems.at[1]
        ),
        pltpu.make_async_copy(e_ref.at[pl.ds(QUARTER, HALF), pl.ds(0, 8), :], edge_e.at[1], sems.at[2]),
        pltpu.make_async_copy(cel_ref.at[pl.ds(ROWS - 8, 8), :], cels.at[0], sems.at[3]),
        pltpu.make_async_copy(mask_ref.at[pl.ds(ROWS - 8, 8), :], masks.at[0], sems.at[4]),
        pltpu.make_async_copy(cel_ref.at[pl.ds(0, 8), :], cels.at[1], sems.at[5]),
        pltpu.make_async_copy(mask_ref.at[pl.ds(0, 8), :], masks.at[1], sems.at[6]),
    ]
    for copy in copies:
        copy.start()
    ahead = pltpu.make_async_copy(e_ref.at[pl.ds(QUARTER, HALF)], up_e_ref, sems.at[7])
    ahead.start()
    sub, lane = iotas()
    speed = speed_of(at_ref)
    odd = at_ref[0] & 1
    for copy in copies:
        copy.wait()
    for side, dirs, row, sx in ((0, DOWNWARD, 7, 1), (1, UPWARD, 0, -1)):
        cw = [cels[side, :, lane_tile(j)] * masks[side, :, lane_tile(j)].astype(F32) for j in range(LTILES)]
        out = odd if side == 0 else 1 - odd
        for i, k in enumerate(dirs):
            ax, ay = speed * ABS_X[k], speed * ABS_Y[k]
            energy = [edge_e[side, i, :, lane_tile(j)] for j in range(LTILES)]
            flux = [cw[j] * energy[j] for j in range(LTILES)]
            after = advance([energy], [flux], ax, ay, sx, 1 if SIN[k] > 0 else -1, sub, lane)[0]
            for j in range(LTILES):
                rim_ref[out, pl.ds(j * NDIR + i, 1), :] = flux[j][row : row + 1]
                rim_ref[out, pl.ds(j * NDIR + HALF + i, 1), :] = (cw[j] * after[j])[row : row + 1]
    near_ref[...] = rim_ref[0]
    far_ref[...] = rim_ref[1]
    ahead.wait()


def propagate(speed, dirs, sx, e_ref, cw_ref, table_ref, e2_ref, sum_ref):
    sub, lane = iotas()
    for i, k in enumerate(dirs):
        table_ref[0, i] = speed * ABS_X[k]
        table_ref[1, i] = speed * ABS_Y[k]

    for half, sy in ((0, 1), (1, -1)):

        def body(piece, carry):
            total = None
            for d in range(PIECE):
                i = half * QUARTER + piece * PIECE + d
                ax, ay = table_ref[0, i], table_ref[1, i]
                cw = [[cw_ref[pl.ds(8 * r, 8), lane_tile(j)] for j in range(LTILES)] for r in range(STILES)]
                energy = [[e_ref[i, pl.ds(8 * r, 8), lane_tile(j)] for j in range(LTILES)] for r in range(STILES)]
                for _ in range(2):
                    flux = [[cw[r][j] * energy[r][j] for j in range(LTILES)] for r in range(STILES)]
                    energy = advance(energy, flux, ax, ay, sx, sy, sub, lane)
                for r in range(STILES):
                    for j in range(LTILES):
                        e2_ref[j, pl.ds(pl.multiple_of(i * ROWS, 8) + 8 * r, 8), :] = energy[r][j]
                total = energy if total is None else [[t + e for t, e in zip(x, y)] for x, y in zip(total, energy)]
            for r in range(STILES):
                for j in range(LTILES):
                    sum_ref[j, pl.ds(8 * r, 8), :] += total[r][j]
            return carry

        lax.fori_loop(0, QUARTER // PIECE, body, 0)


def upward_kernel(
    at_ref, e_hbm, e_ref, cel_ref, mask_ref, pass_in, e2_ref, sum_ref, pass_ref, down_e_ref, cw_ref, table_ref, sems
):
    ahead = [
        pltpu.make_async_copy(e_hbm.at[pl.ds(0, QUARTER)], down_e_ref.at[pl.ds(0, QUARTER)], sems.at[0]),
        pltpu.make_async_copy(e_hbm.at[pl.ds(3 * QUARTER, QUARTER)], down_e_ref.at[pl.ds(QUARTER, QUARTER)], sems.at[1]),
    ]
    for copy in ahead:
        copy.start()
    cw_ref[...] = cel_ref[...] * mask_ref[...].astype(F32)
    sum_ref[...] = jnp.zeros_like(sum_ref)
    pass_ref[...] = pass_in[...]
    propagate(speed_of(at_ref), UPWARD, -1, e_ref, cw_ref, table_ref, e2_ref, sum_ref)
    for copy in ahead:
        copy.wait()


def downward_kernel(at_ref, e_ref, cel_ref, mask_ref, sum_in, e2_ref, sum_ref, cw_ref, table_ref):
    cw_ref[...] = cel_ref[...] * mask_ref[...].astype(F32)
    sum_ref[...] = sum_in[...]
    propagate(speed_of(at_ref), DOWNWARD, 1, e_ref, cw_ref, table_ref, e2_ref, sum_ref)


def add_halo(speed, odd, dirs_ref, near_ref, far_ref, halos_ref, cel_ref, mask_ref, up_ref, down_ref, sum_ref):
    halos_ref[1 - odd] = near_ref[...]
    halos_ref[odd] = far_ref[...]
    sub = lax.broadcasted_iota(jnp.int32, (HALF, LANES), 0)
    lane = lax.broadcasted_iota(jnp.int32, (HALF, LANES), 1)
    zero = jnp.zeros((HALF, LANES), F32)
    for side, e2_ref, row, inside in ((0, down_ref, 0, 1), (1, up_ref, ROWS - 1, ROWS - 2)):
        ax, ay = speed * dirs_ref[2 * side, 0:HALF, :], speed * dirs_ref[2 * side + 1, 0:HALF, :]
        first = [ax * halos_ref[side, pl.ds(j * NDIR, HALF), :] for j in range(LTILES)]
        flux = [
            first[j] * (cel_ref[row : row + 1, lane_tile(j)] * mask_ref[row : row + 1, lane_tile(j)].astype(F32))
            for j in range(LTILES)
        ]
        right = [pltpu.roll(f, 1, 1) for f in flux]
        left = [pltpu.roll(f, LANES - 1, 1) for f in flux]
        for j in range(LTILES):
            r = jnp.where(lane == 0, right[j - 1] if j > 0 else zero, right[j])
            l = jnp.where(lane == LANES - 1, left[j + 1] if j + 1 < LTILES else zero, left[j])
            shifted = jnp.where(sub < QUARTER, r, l)
            outer = first[j] - (ax + ay) * flux[j] + ax * halos_ref[side, pl.ds(j * NDIR + HALF, HALF), :] + ay * shifted
            inner = ax * flux[j]
            for at, part in ((row, outer), (inside, inner)):
                for b in range(0, HALF, 8):
                    n = min(8, HALF - b)
                    cut = pl.ds(b * ROWS + at, n, stride=ROWS)
                    e2_ref[j, cut, :] = e2_ref[j, cut, :] + part[b : b + n]
                if sum_ref is not None:
                    wet = mask_ref[at : at + 1, lane_tile(j)].astype(F32)
                    sum_ref[j, at : at + 1, :] += wet * jnp.sum(part, axis=0, keepdims=True)


def rim_kernel(
    at_ref, dirs_ref, up_in, down_in, sum_in, near_ref, far_ref, cel_ref, mask_ref,
    up_ref, down_ref, sum_ref, halos_ref,
):
    del up_in, down_in
    for j in range(LTILES):
        sum_ref[j] = sum_in[j] * mask_ref[:, lane_tile(j)].astype(F32)
    add_halo(
        speed_of(at_ref), at_ref[0] & 1, dirs_ref, near_ref, far_ref, halos_ref, cel_ref, mask_ref, up_ref, down_ref, sum_ref
    )


def grow(j, speed, up_ref, down_ref, mask_ref, turn_ref, wind_ref, angle_ref, grown_ref):
    cols = pl.ds(pl.multiple_of(j * LANES, LANES), LANES)
    wet = mask_ref[:, cols].astype(F32)
    turn = turn_ref[:, cols] * speed
    wind = wind_ref[:, cols]
    angle = angle_ref[:, cols]
    stay = wet * (1.0 - jnp.abs(turn))
    from_low = wet * jnp.maximum(turn, 0.0)
    from_high = wet * jnp.maximum(-turn, 0.0)
    cosine = jnp.cos(angle)
    sine = jnp.sin(angle)
    gain = (0.3 * speed) * wind
    force = wet * 0.05 * wind * wind

    def load(k):
        k = k % NDIR
        ref, i = (up_ref, k - QUARTER) if k in UPWARD else (down_ref, DOWNWARD.index(k))
        return ref[j, pl.ds(i * ROWS, ROWS), :]

    low, here = load(NDIR - 1), load(0)
    for k in range(NDIR):
        high = load(k + 1)
        refracted = here * stay + low * from_low + high * from_high
        s = jnp.maximum(cosine * COS[k] + sine * SIN[k], 0.0)
        s = s * s
        grown_ref[j, pl.ds(k * STEP, ROWS), :] = refracted * (1.0 + gain * s) + force * s
        low, here = here, high


def grow_kernel(
    at_ref, picked_hbm, up_ref, down_ref, sum_ref, mask_ref, turn_ref, wind_ref, angle_ref,
    out_ref, grown_ref, send_ref, picked_ref, to_ref, sems,
):
    speed = speed_of(at_ref)
    fetch = pltpu.make_async_copy(picked_hbm, picked_ref, sems.at[1])
    fetch.start()

    def invert(g, carry):
        for d in range(8):
            to_ref[picked_ref[g * 8 + d]] = g * 8 + d
        return carry

    rows_ref = send_ref.reshape(DEVICES * SLOT, LANES)

    def tiles(j, carry):
        grow(j, speed, up_ref, down_ref, mask_ref, turn_ref, wind_ref, angle_ref, grown_ref)

        @pl.when(j == 0)
        def _():
            fetch.wait()
            lax.fori_loop(0, DEVICES // 8, invert, 0)

        def pack(g, carry):
            for r in range(8):
                row = g * 8 + r
                at = (j * ROWS + row) * SLOT
                for b in range(0, NDIR, 8):
                    n = min(8, NDIR - b)
                    rows_ref[pl.ds(at + b, n), :] = grown_ref[j, pl.ds(b * STEP + row, n, stride=STEP), :]
                rows_ref[pl.ds(at + NDIR, 1), :] = sum_ref[j, pl.ds(row, 1), :]
                to = to_ref[row * LTILES + j] * SLOT
                pltpu.make_async_copy(send_ref.at[pl.ds(at, SLOT)], out_ref.at[pl.ds(to, SLOT)], sems.at[0]).start()
            return carry

        lax.fori_loop(0, ROWS // 8, pack, 0)
        return carry

    lax.fori_loop(0, LTILES, tiles, 0)
    pltpu.make_async_copy(send_ref, out_ref, sems.at[0]).wait()


def again_kernel(
    at_ref, dirs_ref, e_hbm, near_ref, far_ref, cel_ref, mask_ref, turn_ref, wind_ref, angle_ref,
    grown_hbm, grown_ref, up_e, down_e, up_ref, down_ref, sum_ref, halos_ref, cw_ref, table_ref, sems,
):
    copies = [
        pltpu.make_async_copy(e_hbm.at[pl.ds(QUARTER, HALF)], up_e, sems.at[0]),
        pltpu.make_async_copy(e_hbm.at[pl.ds(0, QUARTER)], down_e.at[pl.ds(0, QUARTER)], sems.at[1]),
        pltpu.make_async_copy(e_hbm.at[pl.ds(3 * QUARTER, QUARTER)], down_e.at[pl.ds(QUARTER, QUARTER)], sems.at[2]),
    ]
    for copy in copies:
        copy.start()
    speed = speed_of(at_ref)
    cw_ref[...] = cel_ref[...] * mask_ref[...].astype(F32)
    sum_ref[...] = jnp.zeros_like(sum_ref)
    for copy in copies:
        copy.wait()
    propagate(speed, UPWARD, -1, up_e, cw_ref, table_ref, up_ref, sum_ref)
    propagate(speed, DOWNWARD, 1, down_e, cw_ref, table_ref, down_ref, sum_ref)
    add_halo(speed, at_ref[0] & 1, dirs_ref, near_ref, far_ref, halos_ref, cel_ref, mask_ref, up_ref, down_ref, None)

    def tiles(j, carry):
        grow(j, speed, up_ref, down_ref, mask_ref, turn_ref, wind_ref, angle_ref, grown_ref)
        return carry

    lax.fori_loop(0, LTILES, tiles, 0)
    store = pltpu.make_async_copy(grown_ref, grown_hbm, sems.at[0])
    store.start()
    store.wait()


def home_kernel(at_ref, grown_ref, mine_ref, other_ref, out_ref, stage_ref, scale_ref, sems):
    speed = speed_of(at_ref)
    for j in range(LTILES):
        mean = (mine_ref[j] + other_ref[j]) * (1.0 / NBINS)
        scale_ref[j] = 1.0 / (1.0 + (2.0 * speed * speed) * mean / (1.0 + mean))
    copies = []
    for part in range(4):
        for j in range(LTILES):
            scale = scale_ref[j]
            for k in range(part * QUARTER, (part + 1) * QUARTER):
                stage_ref[k, :, lane_tile(j)] = grown_ref[j, pl.ds(k * STEP, ROWS), :] * scale
        cut = pl.ds(part * QUARTER, QUARTER)
        copies.append(pltpu.make_async_copy(stage_ref.at[cut], out_ref.at[cut], sems.at[part]))
        copies[-1].start()
    for copy in copies:
        copy.wait()


def owner_kernel(slots_ref, factor_ref, got_ref, out_ref, stage_ref, scale_ref, sems):
    copies = []
    for b in range(OWN):
        sums = got_ref[pl.ds(b * SLOT + NDIR, NFREQ, stride=OWN * SLOT), :]
        mean = jnp.sum(sums, axis=0, keepdims=True) * (1.0 / NBINS)
        scale_ref[b] = 1.0 / (1.0 + factor_ref[...] * mean / (1.0 + mean))
    for b in range(OWN):
        for s in range(NFREQ):
            stage_ref[b, pl.ds(s * NDIR, NDIR), :] = (
                got_ref[pl.ds((s * OWN + b) * SLOT, NDIR), :] * scale_ref[b, s : s + 1, :]
            )
        copies.append(pltpu.make_async_copy(stage_ref.at[b], out_ref.at[slots_ref[b]], sems.at[b]))
        copies[-1].start()
    for copy in copies:
        copy.wait()


def shards(spectrum, land_mask, celerity, turning, wind_speed, wind_dir, tile_order):
    band = lax.axis_index("space")
    me = lax.axis_index(("spec", "space"))
    at = me.astype(jnp.int32).reshape(1)
    space_count = lax.axis_size("space")
    spec_count = lax.axis_size("spec")
    shape = jax.ShapeDtypeStruct

    planes = shape((HALF, ROWS, COLS), F32)
    halves = shape((LTILES, HALF * ROWS, LANES), F32)
    rims = shape((LTILES * NDIR, LANES), F32)
    summed = shape((LTILES, ROWS, LANES), F32)
    near_rim, far_rim, up_e = pl.pallas_call(
        edge_kernel,
        out_shape=(rims, rims, planes),
        in_specs=[SMEM_SPEC] + [HBM_SPEC] * 3,
        out_specs=(VMEM_SPEC,) * 3,
        scratch_shapes=[
            pltpu.VMEM((2, HALF, 8, COLS), F32),
            pltpu.VMEM((2, 8, COLS), F32),
            pltpu.VMEM((2, 8, COLS), jnp.int32),
            pltpu.VMEM((2, LTILES * NDIR, LANES), F32),
            pltpu.SemaphoreType.DMA((8,)),
        ],
        compiler_params=PARAMS,
        name="edges",
    )(at, in_hbm(spectrum), in_hbm(celerity), in_hbm(land_mask))
    within = [(i, i ^ 1) for i in range(space_count)]
    across = [(i, i + 1) for i in range(1, space_count - 1, 2)]
    across = across + [(b, a) for a, b in across]
    far = lax.ppermute(far_rim, "space", across)
    scratch = [pltpu.VMEM((ROWS, COLS), F32), pltpu.SMEM((2, HALF), F32)]
    up_e2, sums, near_rim, down_e = pl.pallas_call(
        upward_kernel,
        out_shape=(halves, summed, rims, planes),
        in_specs=[SMEM_SPEC, HBM_SPEC] + [VMEM_SPEC] * 4,
        out_specs=(VMEM_SPEC,) * 4,
        scratch_shapes=scratch + [pltpu.SemaphoreType.DMA((2,))],
        compiler_params=PARAMS,
        name="upward",
    )(at, in_hbm(spectrum), up_e, celerity, land_mask, near_rim)
    near = lax.ppermute(near_rim, "space", within)
    down_e2, sums = pl.pallas_call(
        downward_kernel,
        out_shape=(halves, summed),
        in_specs=[SMEM_SPEC] + [VMEM_SPEC] * 4,
        out_specs=(VMEM_SPEC,) * 2,
        scratch_shapes=scratch,
        compiler_params=PARAMS,
        name="downward",
    )(at, down_e, celerity, land_mask, sums)

    per_band = ROWS * LTILES
    order = tile_order.reshape(DEVICES, OWN)
    picked = jnp.sum(jnp.where(order // per_band == band, order % per_band, 0), axis=1).astype(jnp.int32)
    own = lax.dynamic_slice_in_dim(order, me, 1, 0).reshape(OWN) // per_band
    slots = jnp.sum(
        jnp.where(own[None, :] == jnp.arange(OWN)[:, None], jnp.arange(OWN)[None, :], 0), axis=1
    ).astype(jnp.int32)

    table = np.zeros((4, EDGE_PAD, LANES), np.float32)
    for i, dirs in enumerate((DOWNWARD, UPWARD)):
        table[2 * i, :HALF] = np.array([ABS_X[k] for k in dirs], np.float32)[:, None]
        table[2 * i + 1, :HALF] = np.array([ABS_Y[k] for k in dirs], np.float32)[:, None]
    table = jnp.asarray(table)
    up_e2, down_e2, sums = pl.pallas_call(
        rim_kernel,
        out_shape=(halves, halves, summed),
        in_specs=[SMEM_SPEC] + [VMEM_SPEC] * 8,
        out_specs=(VMEM_SPEC,) * 3,
        scratch_shapes=[pltpu.VMEM((2, LTILES * NDIR, LANES), F32)],
        input_output_aliases={2: 0, 3: 1},
        compiler_params=PARAMS,
        name="rims",
    )(at, table, up_e2, down_e2, sums, near, far, celerity, land_mask)

    send = pl.pallas_call(
        grow_kernel,
        out_shape=pltpu.HBM((DEVICES * SLOT, 1, LANES), F32),
        in_specs=[SMEM_SPEC, ANY_SPEC] + [VMEM_SPEC] * 7,
        out_specs=HBM_SPEC,
        scratch_shapes=[
            pltpu.VMEM((LTILES, GROWN, LANES), F32),
            pltpu.VMEM((DEVICES * SLOT, 1, LANES), F32),
            pltpu.SMEM((DEVICES,), jnp.int32),
            pltpu.SMEM((DEVICES,), jnp.int32),
            pltpu.SemaphoreType.DMA((2,)),
        ],
        compiler_params=PARAMS,
        name="grow",
    )(at, picked, up_e2, down_e2, sums, land_mask, turning, wind_speed, wind_dir)

    def over_spec(x, masks):
        return [lax.ppermute(x, "spec", [(i, i ^ n) for i in range(spec_count)]) for n in masks]

    (pair,) = over_spec(sums, (1,))
    send, pair = lax.optimization_barrier((send, pair))
    twos = sums + pair
    got = lax.all_to_all(
        send.reshape(DEVICES, SLOT, 1, LANES), ("spec", "space"), split_axis=0, concat_axis=0, tiled=True
    ).reshape(DEVICES * SLOT, LANES)
    fours = over_spec(twos, (3, 12, 15))

    near, far, pair = lax.optimization_barrier((near, far, pair))
    grown = pl.pallas_call(
        again_kernel,
        out_shape=pltpu.HBM((LTILES, GROWN, LANES), F32),
        in_specs=[SMEM_SPEC, VMEM_SPEC, HBM_SPEC] + [VMEM_SPEC] * 7,
        out_specs=HBM_SPEC,
        scratch_shapes=[pltpu.VMEM((LTILES, GROWN, LANES), F32)]
        + [pltpu.VMEM((HALF, ROWS, COLS), F32)] * 2
        + [pltpu.VMEM((LTILES, HALF * ROWS, LANES), F32)] * 2
        + [pltpu.VMEM((LTILES, ROWS, LANES), F32), pltpu.VMEM((2, LTILES * NDIR, LANES), F32)]
        + scratch
        + [pltpu.SemaphoreType.DMA((3,))],
        compiler_params=PARAMS,
        name="again",
    )(at, table, in_hbm(spectrum), near, far, celerity, land_mask, turning, wind_speed, wind_dir)

    fours[0], grown = lax.optimization_barrier((fours[0], grown))
    eights = twos + fours[0] + fours[1] + fours[2]
    (other,) = over_spec(eights, (4,))

    factor = jnp.asarray(np.repeat(2.0 * SPEED[:, None] * SPEED[:, None], LANES, axis=1), F32)
    tile_spectra = pl.pallas_call(
        owner_kernel,
        out_shape=shape((OWN, NBINS, LANES), F32),
        in_specs=[SMEM_SPEC] + [VMEM_SPEC] * 2,
        out_specs=HBM_SPEC,
        scratch_shapes=[
            pltpu.VMEM((OWN, NBINS, LANES), F32),
            pltpu.VMEM((OWN, NFREQ, LANES), F32),
            pltpu.SemaphoreType.DMA((OWN,)),
        ],
        compiler_params=PARAMS,
        name="owned",
    )(slots, factor, got)

    other, tile_spectra = lax.optimization_barrier((other, tile_spectra))
    spectrum_next = pl.pallas_call(
        home_kernel,
        out_shape=shape((NDIR, ROWS, COLS), F32),
        in_specs=[SMEM_SPEC] + [VMEM_SPEC] * 3,
        out_specs=HBM_SPEC,
        scratch_shapes=[
            pltpu.VMEM((NDIR, ROWS, COLS), F32),
            pltpu.VMEM((LTILES, ROWS, LANES), F32),
            pltpu.SemaphoreType.DMA((4,)),
        ],
        compiler_params=PARAMS,
        name="home",
    )(at, grown, eights, other)
    return spectrum_next, tile_spectra


def solution(mesh):
    return jax.shard_map(
        shards,
        mesh=mesh,
        in_specs=(
            P("spec", "space", None),
            P("space", None),
            P("space", None),
            P("space", None),
            P("space", None),
            P("space", None),
            P(),
        ),
        out_specs=(P("spec", "space", None), P(("spec", "space"), None, None)),
        check_vma=False,
    )
```

```python
import math

import jax
import jax.numpy as jnp
import numpy as np
from jax import lax
from jax.experimental import pallas as pl
from jax.experimental.pallas import tpu as pltpu
from jax.sharding import PartitionSpec as P

NDIR = 36
NFREQ = 16
NBINS = NDIR * NFREQ
ROWS = 32
COLS = 512
LANES = 128
LTILES = COLS // LANES
STILES = ROWS // 8
DEVICES = 128
OWN = 8
SLOT = NDIR + 1
QUARTER = NDIR // 4
HALF = NDIR // 2
STEP = ROWS + 1
GROWN = (SLOT * STEP + 7) // 8 * 8
EDGE_PAD = 24
PIECE = 3
FREQ_RATIO = 1.1
COURANT = 0.45

THETA = [2.0 * math.pi * (k + 0.5) / NDIR for k in range(NDIR)]
COS = [float(np.float32(math.cos(t))) for t in THETA]
SIN = [float(np.float32(math.sin(t))) for t in THETA]
ABS_X = [float(np.float32(COURANT * abs(math.cos(t)))) for t in THETA]
ABS_Y = [float(np.float32(COURANT * abs(math.sin(t)))) for t in THETA]
SPEED = np.array([FREQ_RATIO ** (-i) for i in range(NFREQ)], np.float32)
DOWNWARD = list(range(QUARTER)) + list(range(3 * QUARTER, NDIR))
UPWARD = list(range(QUARTER, 3 * QUARTER))

SMEM_SPEC = pl.BlockSpec(memory_space=pltpu.SMEM)
VMEM_SPEC = pl.BlockSpec(memory_space=pltpu.VMEM)
HBM_SPEC = pl.BlockSpec(memory_space=pltpu.HBM)
ANY_SPEC = pl.BlockSpec(memory_space=pl.ANY)
PARAMS = pltpu.CompilerParams(vmem_limit_bytes=16 * 1024 * 1024)
F32 = jnp.float32


def speed_of(at_ref):
    index = at_ref[0] >> 3
    speed = jnp.float32(1.0)
    for bit in (1, 2, 4, 8):
        speed = speed * jnp.where((index & bit) != 0, jnp.float32(FREQ_RATIO ** (-bit)), jnp.float32(1.0))
    return speed


def in_hbm(x):
    return pltpu.with_memory_space_constraint(x, pltpu.HBM)


def lane_tile(j):
    return pl.ds(j * LANES, LANES)


def iotas():
    return (lax.broadcasted_iota(jnp.int32, (8, LANES), 0), lax.broadcasted_iota(jnp.int32, (8, LANES), 1))


def column_shift(tiles, sign, lane):
    edge = 0 if sign > 0 else LANES - 1
    turned = [pltpu.roll(t, 1 if sign > 0 else LANES - 1, 1) for t in tiles]
    zero = jnp.zeros_like(tiles[0])
    out = []
    for j in range(len(tiles)):
        at = j - sign
        out.append(jnp.where(lane == edge, turned[at] if 0 <= at < len(tiles) else zero, turned[j]))
    return out


def row_shift(tiles, sign, sub):
    edge = 0 if sign > 0 else 7
    turned = [pltpu.roll(t, 1 if sign > 0 else 7, 0) for t in tiles]
    zero = jnp.zeros_like(tiles[0])
    out = []
    for i in range(len(tiles)):
        at = i - sign
        out.append(jnp.where(sub == edge, turned[at] if 0 <= at < len(tiles) else zero, turned[i]))
    return out


def advance(energy, flux, ax, ay, sx, sy, sub, lane):
    n = len(energy)
    by_col = [column_shift(flux[i], sy, lane) for i in range(n)]
    total = ax + ay
    out = [[None] * LTILES for _ in range(n)]
    for j in range(LTILES):
        by_row = row_shift([flux[i][j] for i in range(n)], sx, sub)
        for i in range(n):
            out[i][j] = energy[i][j] - total * flux[i][j] + ax * by_row[i] + ay * by_col[i][j]
    return out


def edge_kernel(at_ref, e_ref, cel_ref, mask_ref, near_ref, far_ref, up_e_ref, edge_e, cels, masks, rim_ref, sems):
    copies = [
        pltpu.make_async_copy(e_ref.at[pl.ds(0, QUARTER), pl.ds(ROWS - 8, 8), :], edge_e.at[0, pl.ds(0, QUARTER)], sems.at[0]),
        pltpu.make_async_copy(
            e_ref.at[pl.ds(3 * QUARTER, QUARTER), pl.ds(ROWS - 8, 8), :], edge_e.at[0, pl.ds(QUARTER, QUARTER)], sems.at[1]
        ),
        pltpu.make_async_copy(e_ref.at[pl.ds(QUARTER, HALF), pl.ds(0, 8), :], edge_e.at[1], sems.at[2]),
        pltpu.make_async_copy(cel_ref.at[pl.ds(ROWS - 8, 8), :], cels.at[0], sems.at[3]),
        pltpu.make_async_copy(mask_ref.at[pl.ds(ROWS - 8, 8), :], masks.at[0], sems.at[4]),
        pltpu.make_async_copy(cel_ref.at[pl.ds(0, 8), :], cels.at[1], sems.at[5]),
        pltpu.make_async_copy(mask_ref.at[pl.ds(0, 8), :], masks.at[1], sems.at[6]),
    ]
    for copy in copies:
        copy.start()
    ahead = pltpu.make_async_copy(e_ref.at[pl.ds(QUARTER, HALF)], up_e_ref, sems.at[7])
    ahead.start()
    sub, lane = iotas()
    speed = speed_of(at_ref)
    odd = at_ref[0] & 1
    for copy in copies:
        copy.wait()
    for side, dirs, row, sx in ((0, DOWNWARD, 7, 1), (1, UPWARD, 0, -1)):
        cw = [cels[side, :, lane_tile(j)] * masks[side, :, lane_tile(j)].astype(F32) for j in range(LTILES)]
        out = odd if side == 0 else 1 - odd
        for i, k in enumerate(dirs):
            ax, ay = speed * ABS_X[k], speed * ABS_Y[k]
            energy = [edge_e[side, i, :, lane_tile(j)] for j in range(LTILES)]
            flux = [cw[j] * energy[j] for j in range(LTILES)]
            after = advance([energy], [flux], ax, ay, sx, 1 if SIN[k] > 0 else -1, sub, lane)[0]
            for j in range(LTILES):
                rim_ref[out, pl.ds(j * NDIR + i, 1), :] = flux[j][row : row + 1]
                rim_ref[out, pl.ds(j * NDIR + HALF + i, 1), :] = (cw[j] * after[j])[row : row + 1]
    near_ref[...] = rim_ref[0]
    far_ref[...] = rim_ref[1]
    ahead.wait()


def propagate(speed, dirs, sx, e_ref, cw_ref, table_ref, e2_ref, sum_ref):
    sub, lane = iotas()
    for i, k in enumerate(dirs):
        table_ref[0, i] = speed * ABS_X[k]
        table_ref[1, i] = speed * ABS_Y[k]

    for half, sy in ((0, 1), (1, -1)):

        def body(piece, carry):
            total = None
            for d in range(PIECE):
                i = half * QUARTER + piece * PIECE + d
                ax, ay = table_ref[0, i], table_ref[1, i]
                cw = [[cw_ref[pl.ds(8 * r, 8), lane_tile(j)] for j in range(LTILES)] for r in range(STILES)]
                energy = [[e_ref[i, pl.ds(8 * r, 8), lane_tile(j)] for j in range(LTILES)] for r in range(STILES)]
                for _ in range(2):
                    flux = [[cw[r][j] * energy[r][j] for j in range(LTILES)] for r in range(STILES)]
                    energy = advance(energy, flux, ax, ay, sx, sy, sub, lane)
                for r in range(STILES):
                    for j in range(LTILES):
                        e2_ref[j, pl.ds(pl.multiple_of(i * ROWS, 8) + 8 * r, 8), :] = energy[r][j]
                total = energy if total is None else [[t + e for t, e in zip(x, y)] for x, y in zip(total, energy)]
            for r in range(STILES):
                for j in range(LTILES):
                    sum_ref[j, pl.ds(8 * r, 8), :] += total[r][j]
            return carry

        lax.fori_loop(0, QUARTER // PIECE, body, 0)


def upward_kernel(
    at_ref, e_hbm, e_ref, cel_ref, mask_ref, pass_in, e2_ref, sum_ref, pass_ref, down_e_ref, cw_ref, table_ref, sems
):
    ahead = [
        pltpu.make_async_copy(e_hbm.at[pl.ds(0, QUARTER)], down_e_ref.at[pl.ds(0, QUARTER)], sems.at[0]),
        pltpu.make_async_copy(e_hbm.at[pl.ds(3 * QUARTER, QUARTER)], down_e_ref.at[pl.ds(QUARTER, QUARTER)], sems.at[1]),
    ]
    for copy in ahead:
        copy.start()
    cw_ref[...] = cel_ref[...] * mask_ref[...].astype(F32)
    sum_ref[...] = jnp.zeros_like(sum_ref)
    pass_ref[...] = pass_in[...]
    propagate(speed_of(at_ref), UPWARD, -1, e_ref, cw_ref, table_ref, e2_ref, sum_ref)
    for copy in ahead:
        copy.wait()


def downward_kernel(at_ref, e_ref, cel_ref, mask_ref, sum_in, e2_ref, sum_ref, cw_ref, table_ref):
    cw_ref[...] = cel_ref[...] * mask_ref[...].astype(F32)
    sum_ref[...] = sum_in[...]
    propagate(speed_of(at_ref), DOWNWARD, 1, e_ref, cw_ref, table_ref, e2_ref, sum_ref)


def add_halo(speed, odd, dirs_ref, near_ref, far_ref, halos_ref, cel_ref, mask_ref, up_ref, down_ref, sum_ref):
    halos_ref[1 - odd] = near_ref[...]
    halos_ref[odd] = far_ref[...]
    sub = lax.broadcasted_iota(jnp.int32, (HALF, LANES), 0)
    lane = lax.broadcasted_iota(jnp.int32, (HALF, LANES), 1)
    zero = jnp.zeros((HALF, LANES), F32)
    for side, e2_ref, row, inside in ((0, down_ref, 0, 1), (1, up_ref, ROWS - 1, ROWS - 2)):
        ax, ay = speed * dirs_ref[2 * side, 0:HALF, :], speed * dirs_ref[2 * side + 1, 0:HALF, :]
        first = [ax * halos_ref[side, pl.ds(j * NDIR, HALF), :] for j in range(LTILES)]
        flux = [
            first[j] * (cel_ref[row : row + 1, lane_tile(j)] * mask_ref[row : row + 1, lane_tile(j)].astype(F32))
            for j in range(LTILES)
        ]
        right = [pltpu.roll(f, 1, 1) for f in flux]
        left = [pltpu.roll(f, LANES - 1, 1) for f in flux]
        for j in range(LTILES):
            r = jnp.where(lane == 0, right[j - 1] if j > 0 else zero, right[j])
            l = jnp.where(lane == LANES - 1, left[j + 1] if j + 1 < LTILES else zero, left[j])
            shifted = jnp.where(sub < QUARTER, r, l)
            outer = first[j] - (ax + ay) * flux[j] + ax * halos_ref[side, pl.ds(j * NDIR + HALF, HALF), :] + ay * shifted
            inner = ax * flux[j]
            for at, part in ((row, outer), (inside, inner)):
                for b in range(0, HALF - 2, 8):
                    cut = pl.ds(b * ROWS + at, 8, stride=ROWS)
                    e2_ref[j, cut, :] = e2_ref[j, cut, :] + part[b : b + 8]
                for b in range(HALF - 2, HALF):
                    e2_ref[j, b * ROWS + at : b * ROWS + at + 1, :] += part[b : b + 1]
                if sum_ref is not None:
                    wet = mask_ref[at : at + 1, lane_tile(j)].astype(F32)
                    sum_ref[j, at : at + 1, :] += wet * jnp.sum(part, axis=0, keepdims=True)


def rim_kernel(
    at_ref, dirs_ref, up_in, down_in, sum_in, near_ref, far_ref, cel_ref, mask_ref,
    up_ref, down_ref, sum_ref, halos_ref,
):
    del up_in, down_in
    for j in range(LTILES):
        sum_ref[j] = sum_in[j] * mask_ref[:, lane_tile(j)].astype(F32)
    add_halo(
        speed_of(at_ref), at_ref[0] & 1, dirs_ref, near_ref, far_ref, halos_ref, cel_ref, mask_ref, up_ref, down_ref, sum_ref
    )


def grow(j, speed, up_ref, down_ref, mask_ref, turn_ref, wind_ref, angle_ref, grown_ref):
    cols = pl.ds(pl.multiple_of(j * LANES, LANES), LANES)
    wet = mask_ref[:, cols].astype(F32)
    turn = turn_ref[:, cols] * speed
    wind = wind_ref[:, cols]
    angle = angle_ref[:, cols]
    stay = wet * (1.0 - jnp.abs(turn))
    from_low = wet * jnp.maximum(turn, 0.0)
    from_high = wet * jnp.maximum(-turn, 0.0)
    cosine = jnp.cos(angle)
    sine = jnp.sin(angle)
    gain = (0.3 * speed) * wind
    force = wet * 0.05 * wind * wind

    def load(k):
        k = k % NDIR
        ref, i = (up_ref, k - QUARTER) if k in UPWARD else (down_ref, DOWNWARD.index(k))
        return ref[j, pl.ds(i * ROWS, ROWS), :]

    low, here = load(NDIR - 1), load(0)
    for k in range(NDIR):
        high = load(k + 1)
        refracted = here * stay + low * from_low + high * from_high
        s = jnp.maximum(cosine * COS[k] + sine * SIN[k], 0.0)
        s = s * s
        grown_ref[j, pl.ds(k * STEP, ROWS), :] = refracted * (1.0 + gain * s) + force * s
        low, here = here, high


def grow_kernel(
    at_ref, picked_hbm, up_ref, down_ref, sum_ref, mask_ref, turn_ref, wind_ref, angle_ref,
    out_ref, grown_ref, send_ref, picked_ref, to_ref, sems,
):
    speed = speed_of(at_ref)
    fetch = pltpu.make_async_copy(picked_hbm, picked_ref, sems.at[1])
    fetch.start()

    def invert(g, carry):
        for d in range(8):
            to_ref[picked_ref[g * 8 + d]] = g * 8 + d
        return carry

    rows_ref = send_ref.reshape(DEVICES * SLOT, LANES)

    def tiles(j, carry):
        grow(j, speed, up_ref, down_ref, mask_ref, turn_ref, wind_ref, angle_ref, grown_ref)
        grown_ref[j, pl.ds(NDIR * STEP, ROWS), :] = sum_ref[j]

        @pl.when(j == 0)
        def _():
            fetch.wait()
            lax.fori_loop(0, DEVICES // 8, invert, 0)

        def pack(g, carry):
            for r in range(8):
                row = g * 8 + r
                at = (j * ROWS + row) * SLOT
                for b in (0, 8, 16, 24, SLOT - 8):
                    rows_ref[pl.ds(at + b, 8), :] = grown_ref[j, pl.ds(b * STEP + row, 8, stride=STEP), :]
                to = to_ref[row * LTILES + j] * SLOT
                pltpu.make_async_copy(send_ref.at[pl.ds(at, SLOT)], out_ref.at[pl.ds(to, SLOT)], sems.at[0]).start()
            return carry

        lax.fori_loop(0, ROWS // 8, pack, 0)
        return carry

    lax.fori_loop(0, LTILES, tiles, 0)
    pltpu.make_async_copy(send_ref, out_ref, sems.at[0]).wait()


def again_kernel(
    at_ref, dirs_ref, e_hbm, near_ref, far_ref, cel_ref, mask_ref, turn_ref, wind_ref, angle_ref,
    grown_hbm, grown_ref, up_e, down_e, up_ref, down_ref, sum_ref, halos_ref, cw_ref, table_ref, sems,
):
    copies = [
        pltpu.make_async_copy(e_hbm.at[pl.ds(QUARTER, HALF)], up_e, sems.at[0]),
        pltpu.make_async_copy(e_hbm.at[pl.ds(0, QUARTER)], down_e.at[pl.ds(0, QUARTER)], sems.at[1]),
        pltpu.make_async_copy(e_hbm.at[pl.ds(3 * QUARTER, QUARTER)], down_e.at[pl.ds(QUARTER, QUARTER)], sems.at[2]),
    ]
    for copy in copies:
        copy.start()
    speed = speed_of(at_ref)
    cw_ref[...] = cel_ref[...] * mask_ref[...].astype(F32)
    sum_ref[...] = jnp.zeros_like(sum_ref)
    for copy in copies:
        copy.wait()
    propagate(speed, UPWARD, -1, up_e, cw_ref, table_ref, up_ref, sum_ref)
    propagate(speed, DOWNWARD, 1, down_e, cw_ref, table_ref, down_ref, sum_ref)
    add_halo(speed, at_ref[0] & 1, dirs_ref, near_ref, far_ref, halos_ref, cel_ref, mask_ref, up_ref, down_ref, None)

    def tiles(j, carry):
        grow(j, speed, up_ref, down_ref, mask_ref, turn_ref, wind_ref, angle_ref, grown_ref)
        return carry

    lax.fori_loop(0, LTILES, tiles, 0)
    store = pltpu.make_async_copy(grown_ref, grown_hbm, sems.at[0])
    store.start()
    store.wait()


def home_kernel(at_ref, grown_ref, mine_ref, other_ref, out_ref, stage_ref, scale_ref, sems):
    speed = speed_of(at_ref)
    for j in range(LTILES):
        mean = (mine_ref[j] + other_ref[j]) * (1.0 / NBINS)
        scale_ref[j] = 1.0 / (1.0 + (2.0 * speed * speed) * mean / (1.0 + mean))
    copies = []
    for part in range(4):
        for j in range(LTILES):
            scale = scale_ref[j]
            for k in range(part * QUARTER, (part + 1) * QUARTER):
                stage_ref[k, :, lane_tile(j)] = grown_ref[j, pl.ds(k * STEP, ROWS), :] * scale
        cut = pl.ds(part * QUARTER, QUARTER)
        copies.append(pltpu.make_async_copy(stage_ref.at[cut], out_ref.at[cut], sems.at[part]))
        copies[-1].start()
    for copy in copies:
        copy.wait()


def owner_kernel(slots_ref, factor_ref, got_ref, out_ref, stage_ref, scale_ref, sems):
    copies = []
    for b in range(OWN):
        sums = got_ref[pl.ds(b * SLOT + NDIR, NFREQ, stride=OWN * SLOT), :]
        mean = jnp.sum(sums, axis=0, keepdims=True) * (1.0 / NBINS)
        scale_ref[b] = 1.0 / (1.0 + factor_ref[...] * mean / (1.0 + mean))
    for b in range(OWN):
        for s in range(NFREQ):
            stage_ref[b, pl.ds(s * NDIR, NDIR), :] = (
                got_ref[pl.ds((s * OWN + b) * SLOT, NDIR), :] * scale_ref[b, s : s + 1, :]
            )
        copies.append(pltpu.make_async_copy(stage_ref.at[b], out_ref.at[slots_ref[b]], sems.at[b]))
        copies[-1].start()
    for copy in copies:
        copy.wait()


def shards(spectrum, land_mask, celerity, turning, wind_speed, wind_dir, tile_order):
    band = lax.axis_index("space")
    me = lax.axis_index(("spec", "space"))
    at = me.astype(jnp.int32).reshape(1)
    space_count = lax.axis_size("space")
    spec_count = lax.axis_size("spec")
    shape = jax.ShapeDtypeStruct

    planes = shape((HALF, ROWS, COLS), F32)
    halves = shape((LTILES, HALF * ROWS, LANES), F32)
    rims = shape((LTILES * NDIR, LANES), F32)
    summed = shape((LTILES, ROWS, LANES), F32)
    near_rim, far_rim, up_e = pl.pallas_call(
        edge_kernel,
        out_shape=(rims, rims, planes),
        in_specs=[SMEM_SPEC] + [HBM_SPEC] * 3,
        out_specs=(VMEM_SPEC,) * 3,
        scratch_shapes=[
            pltpu.VMEM((2, HALF, 8, COLS), F32),
            pltpu.VMEM((2, 8, COLS), F32),
            pltpu.VMEM((2, 8, COLS), jnp.int32),
            pltpu.VMEM((2, LTILES * NDIR, LANES), F32),
            pltpu.SemaphoreType.DMA((8,)),
        ],
        compiler_params=PARAMS,
        name="edges",
    )(at, in_hbm(spectrum), in_hbm(celerity), in_hbm(land_mask))
    within = [(i, i ^ 1) for i in range(space_count)]
    across = [(i, i + 1) for i in range(1, space_count - 1, 2)]
    across = across + [(b, a) for a, b in across]
    far = lax.ppermute(far_rim, "space", across)
    scratch = [pltpu.VMEM((ROWS, COLS), F32), pltpu.SMEM((2, HALF), F32)]
    up_e2, sums, near_rim, down_e = pl.pallas_call(
        upward_kernel,
        out_shape=(halves, summed, rims, planes),
        in_specs=[SMEM_SPEC, HBM_SPEC] + [VMEM_SPEC] * 4,
        out_specs=(VMEM_SPEC,) * 4,
        scratch_shapes=scratch + [pltpu.SemaphoreType.DMA((2,))],
        compiler_params=PARAMS,
        name="upward",
    )(at, in_hbm(spectrum), up_e, celerity, land_mask, near_rim)
    near = lax.ppermute(near_rim, "space", within)
    down_e2, sums = pl.pallas_call(
        downward_kernel,
        out_shape=(halves, summed),
        in_specs=[SMEM_SPEC] + [VMEM_SPEC] * 4,
        out_specs=(VMEM_SPEC,) * 2,
        scratch_shapes=scratch,
        compiler_params=PARAMS,
        name="downward",
    )(at, down_e, celerity, land_mask, sums)

    per_band = ROWS * LTILES
    order = tile_order.reshape(DEVICES, OWN)
    picked = jnp.sum(jnp.where(order // per_band == band, order % per_band, 0), axis=1).astype(jnp.int32)
    own = lax.dynamic_slice_in_dim(order, me, 1, 0).reshape(OWN) // per_band
    slots = jnp.sum(
        jnp.where(own[None, :] == jnp.arange(OWN)[:, None], jnp.arange(OWN)[None, :], 0), axis=1
    ).astype(jnp.int32)

    table = np.zeros((4, EDGE_PAD, LANES), np.float32)
    for i, dirs in enumerate((DOWNWARD, UPWARD)):
        table[2 * i, :HALF] = np.array([ABS_X[k] for k in dirs], np.float32)[:, None]
        table[2 * i + 1, :HALF] = np.array([ABS_Y[k] for k in dirs], np.float32)[:, None]
    table = jnp.asarray(table)
    up_e2, down_e2, sums = pl.pallas_call(
        rim_kernel,
        out_shape=(halves, halves, summed),
        in_specs=[SMEM_SPEC] + [VMEM_SPEC] * 8,
        out_specs=(VMEM_SPEC,) * 3,
        scratch_shapes=[pltpu.VMEM((2, LTILES * NDIR, LANES), F32)],
        input_output_aliases={2: 0, 3: 1},
        compiler_params=PARAMS,
        name="rims",
    )(at, table, up_e2, down_e2, sums, near, far, celerity, land_mask)

    send = pl.pallas_call(
        grow_kernel,
        out_shape=pltpu.HBM((DEVICES * SLOT, 1, LANES), F32),
        in_specs=[SMEM_SPEC, ANY_SPEC] + [VMEM_SPEC] * 7,
        out_specs=HBM_SPEC,
        scratch_shapes=[
            pltpu.VMEM((LTILES, GROWN, LANES), F32),
            pltpu.VMEM((DEVICES * SLOT, 1, LANES), F32),
            pltpu.SMEM((DEVICES,), jnp.int32),
            pltpu.SMEM((DEVICES,), jnp.int32),
            pltpu.SemaphoreType.DMA((2,)),
        ],
        compiler_params=PARAMS,
        name="grow",
    )(at, picked, up_e2, down_e2, sums, land_mask, turning, wind_speed, wind_dir)

    def over_spec(x, masks):
        return [lax.ppermute(x, "spec", [(i, i ^ n) for i in range(spec_count)]) for n in masks]

    (pair,) = over_spec(sums, (1,))
    send, pair = lax.optimization_barrier((send, pair))
    twos = sums + pair
    got = lax.all_to_all(
        send.reshape(DEVICES, SLOT, 1, LANES), ("spec", "space"), split_axis=0, concat_axis=0, tiled=True
    ).reshape(DEVICES * SLOT, LANES)
    fours = over_spec(twos, (3, 12, 15))

    near, far, pair = lax.optimization_barrier((near, far, pair))
    grown = pl.pallas_call(
        again_kernel,
        out_shape=pltpu.HBM((LTILES, GROWN, LANES), F32),
        in_specs=[SMEM_SPEC, VMEM_SPEC, HBM_SPEC] + [VMEM_SPEC] * 7,
        out_specs=HBM_SPEC,
        scratch_shapes=[pltpu.VMEM((LTILES, GROWN, LANES), F32)]
        + [pltpu.VMEM((HALF, ROWS, COLS), F32)] * 2
        + [pltpu.VMEM((LTILES, HALF * ROWS, LANES), F32)] * 2
        + [pltpu.VMEM((LTILES, ROWS, LANES), F32), pltpu.VMEM((2, LTILES * NDIR, LANES), F32)]
        + scratch
        + [pltpu.SemaphoreType.DMA((3,))],
        compiler_params=PARAMS,
        name="again",
    )(at, table, in_hbm(spectrum), near, far, celerity, land_mask, turning, wind_speed, wind_dir)

    fours[0], grown = lax.optimization_barrier((fours[0], grown))
    eights = twos + fours[0] + fours[1] + fours[2]
    (other,) = over_spec(eights, (4,))

    factor = jnp.asarray(np.repeat(2.0 * SPEED[:, None] * SPEED[:, None], LANES, axis=1), F32)
    tile_spectra = pl.pallas_call(
        owner_kernel,
        out_shape=shape((OWN, NBINS, LANES), F32),
        in_specs=[SMEM_SPEC] + [VMEM_SPEC] * 2,
        out_specs=HBM_SPEC,
        scratch_shapes=[
            pltpu.VMEM((OWN, NBINS, LANES), F32),
            pltpu.VMEM((OWN, NFREQ, LANES), F32),
            pltpu.SemaphoreType.DMA((OWN,)),
        ],
        compiler_params=PARAMS,
        name="owned",
    )(slots, factor, got)

    other, tile_spectra = lax.optimization_barrier((other, tile_spectra))
    spectrum_next = pl.pallas_call(
        home_kernel,
        out_shape=shape((NDIR, ROWS, COLS), F32),
        in_specs=[SMEM_SPEC] + [VMEM_SPEC] * 3,
        out_specs=HBM_SPEC,
        scratch_shapes=[
            pltpu.VMEM((NDIR, ROWS, COLS), F32),
            pltpu.VMEM((LTILES, ROWS, LANES), F32),
            pltpu.SemaphoreType.DMA((4,)),
        ],
        compiler_params=PARAMS,
        name="home",
    )(at, grown, eights, other)
    return spectrum_next, tile_spectra


def solution(mesh):
    return jax.shard_map(
        shards,
        mesh=mesh,
        in_specs=(
            P("spec", "space", None),
            P("space", None),
            P("space", None),
            P("space", None),
            P("space", None),
            P("space", None),
            P(),
        ),
        out_specs=(P("spec", "space", None), P(("spec", "space"), None, None)),
        check_vma=False,
    )
```

```python
import math

import jax
import jax.numpy as jnp
import numpy as np
from jax import lax
from jax.experimental import pallas as pl
from jax.experimental.pallas import tpu as pltpu
from jax.sharding import PartitionSpec as P

NDIR = 36
NFREQ = 16
NBINS = NDIR * NFREQ
ROWS = 32
COLS = 512
LANES = 128
LTILES = COLS // LANES
STILES = ROWS // 8
DEVICES = 128
OWN = 8
SLOT = NDIR + 1
QUARTER = NDIR // 4
HALF = NDIR // 2
STEP = ROWS + 1
GROWN = (SLOT * STEP + 7) // 8 * 8
EDGE_PAD = 24
PIECE = 3
FREQ_RATIO = 1.1
COURANT = 0.45

THETA = [2.0 * math.pi * (k + 0.5) / NDIR for k in range(NDIR)]
COS = [float(np.float32(math.cos(t))) for t in THETA]
SIN = [float(np.float32(math.sin(t))) for t in THETA]
ABS_X = [float(np.float32(COURANT * abs(math.cos(t)))) for t in THETA]
ABS_Y = [float(np.float32(COURANT * abs(math.sin(t)))) for t in THETA]
SPEED = np.array([FREQ_RATIO ** (-i) for i in range(NFREQ)], np.float32)
DOWNWARD = list(range(QUARTER)) + list(range(3 * QUARTER, NDIR))
UPWARD = list(range(QUARTER, 3 * QUARTER))

SMEM_SPEC = pl.BlockSpec(memory_space=pltpu.SMEM)
VMEM_SPEC = pl.BlockSpec(memory_space=pltpu.VMEM)
HBM_SPEC = pl.BlockSpec(memory_space=pltpu.HBM)
ANY_SPEC = pl.BlockSpec(memory_space=pl.ANY)
PARAMS = pltpu.CompilerParams(vmem_limit_bytes=16 * 1024 * 1024)
F32 = jnp.float32


def speed_of(at_ref):
    index = at_ref[0] >> 3
    speed = jnp.float32(1.0)
    for bit in (1, 2, 4, 8):
        speed = speed * jnp.where((index & bit) != 0, jnp.float32(FREQ_RATIO ** (-bit)), jnp.float32(1.0))
    return speed


def in_hbm(x):
    return pltpu.with_memory_space_constraint(x, pltpu.HBM)


def lane_tile(j):
    return pl.ds(j * LANES, LANES)


def iotas():
    return (lax.broadcasted_iota(jnp.int32, (8, LANES), 0), lax.broadcasted_iota(jnp.int32, (8, LANES), 1))


def column_shift(tiles, sign, lane):
    edge = 0 if sign > 0 else LANES - 1
    turned = [pltpu.roll(t, 1 if sign > 0 else LANES - 1, 1) for t in tiles]
    zero = jnp.zeros_like(tiles[0])
    out = []
    for j in range(len(tiles)):
        at = j - sign
        out.append(jnp.where(lane == edge, turned[at] if 0 <= at < len(tiles) else zero, turned[j]))
    return out


def row_shift(tiles, sign, sub):
    edge = 0 if sign > 0 else 7
    turned = [pltpu.roll(t, 1 if sign > 0 else 7, 0) for t in tiles]
    zero = jnp.zeros_like(tiles[0])
    out = []
    for i in range(len(tiles)):
        at = i - sign
        out.append(jnp.where(sub == edge, turned[at] if 0 <= at < len(tiles) else zero, turned[i]))
    return out


def advance(energy, flux, ax, ay, sx, sy, sub, lane):
    n = len(energy)
    by_col = [column_shift(flux[i], sy, lane) for i in range(n)]
    total = ax + ay
    out = [[None] * LTILES for _ in range(n)]
    for j in range(LTILES):
        by_row = row_shift([flux[i][j] for i in range(n)], sx, sub)
        for i in range(n):
            out[i][j] = energy[i][j] - total * flux[i][j] + ax * by_row[i] + ay * by_col[i][j]
    return out


def edge_kernel(at_ref, e_ref, cel_ref, mask_ref, near_ref, far_ref, up_e_ref, edge_e, cels, masks, rim_ref, sems):
    copies = [
        pltpu.make_async_copy(e_ref.at[pl.ds(0, QUARTER), pl.ds(ROWS - 8, 8), :], edge_e.at[0, pl.ds(0, QUARTER)], sems.at[0]),
        pltpu.make_async_copy(
            e_ref.at[pl.ds(3 * QUARTER, QUARTER), pl.ds(ROWS - 8, 8), :], edge_e.at[0, pl.ds(QUARTER, QUARTER)], sems.at[1]
        ),
        pltpu.make_async_copy(e_ref.at[pl.ds(QUARTER, HALF), pl.ds(0, 8), :], edge_e.at[1], sems.at[2]),
        pltpu.make_async_copy(cel_ref.at[pl.ds(ROWS - 8, 8), :], cels.at[0], sems.at[3]),
        pltpu.make_async_copy(mask_ref.at[pl.ds(ROWS - 8, 8), :], masks.at[0], sems.at[4]),
        pltpu.make_async_copy(cel_ref.at[pl.ds(0, 8), :], cels.at[1], sems.at[5]),
        pltpu.make_async_copy(mask_ref.at[pl.ds(0, 8), :], masks.at[1], sems.at[6]),
    ]
    for copy in copies:
        copy.start()
    ahead = pltpu.make_async_copy(e_ref.at[pl.ds(QUARTER, HALF)], up_e_ref, sems.at[7])
    ahead.start()
    sub, lane = iotas()
    speed = speed_of(at_ref)
    odd = at_ref[0] & 1
    for copy in copies:
        copy.wait()
    for side, dirs, row, sx in ((0, DOWNWARD, 7, 1), (1, UPWARD, 0, -1)):
        cw = [cels[side, :, lane_tile(j)] * masks[side, :, lane_tile(j)].astype(F32) for j in range(LTILES)]
        out = odd if side == 0 else 1 - odd
        for i, k in enumerate(dirs):
            ax, ay = speed * ABS_X[k], speed * ABS_Y[k]
            energy = [edge_e[side, i, :, lane_tile(j)] for j in range(LTILES)]
            flux = [cw[j] * energy[j] for j in range(LTILES)]
            after = advance([energy], [flux], ax, ay, sx, 1 if SIN[k] > 0 else -1, sub, lane)[0]
            for j in range(LTILES):
                rim_ref[out, pl.ds(j * NDIR + i, 1), :] = flux[j][row : row + 1]
                rim_ref[out, pl.ds(j * NDIR + HALF + i, 1), :] = (cw[j] * after[j])[row : row + 1]
    near_ref[...] = rim_ref[0]
    far_ref[...] = rim_ref[1]
    ahead.wait()


def propagate(speed, dirs, sx, e_ref, cw_ref, table_ref, e2_ref, sum_ref):
    sub, lane = iotas()
    for i, k in enumerate(dirs):
        table_ref[0, i] = speed * ABS_X[k]
        table_ref[1, i] = speed * ABS_Y[k]

    for half, sy in ((0, 1), (1, -1)):

        def body(piece, carry):
            total = None
            for d in range(PIECE):
                i = half * QUARTER + piece * PIECE + d
                ax, ay = table_ref[0, i], table_ref[1, i]
                cw = [[cw_ref[pl.ds(8 * r, 8), lane_tile(j)] for j in range(LTILES)] for r in range(STILES)]
                energy = [[e_ref[i, pl.ds(8 * r, 8), lane_tile(j)] for j in range(LTILES)] for r in range(STILES)]
                for _ in range(2):
                    flux = [[cw[r][j] * energy[r][j] for j in range(LTILES)] for r in range(STILES)]
                    energy = advance(energy, flux, ax, ay, sx, sy, sub, lane)
                for r in range(STILES):
                    for j in range(LTILES):
                        e2_ref[j, pl.ds(pl.multiple_of(i * ROWS, 8) + 8 * r, 8), :] = energy[r][j]
                total = energy if total is None else [[t + e for t, e in zip(x, y)] for x, y in zip(total, energy)]
            for r in range(STILES):
                for j in range(LTILES):
                    sum_ref[j, pl.ds(8 * r, 8), :] += total[r][j]
            return carry

        lax.fori_loop(0, QUARTER // PIECE, body, 0)


def upward_kernel(
    at_ref, e_hbm, e_ref, cel_ref, mask_ref, pass_in, e2_ref, sum_ref, pass_ref, down_e_ref, cw_ref, table_ref, sems
):
    ahead = [
        pltpu.make_async_copy(e_hbm.at[pl.ds(0, QUARTER)], down_e_ref.at[pl.ds(0, QUARTER)], sems.at[0]),
        pltpu.make_async_copy(e_hbm.at[pl.ds(3 * QUARTER, QUARTER)], down_e_ref.at[pl.ds(QUARTER, QUARTER)], sems.at[1]),
    ]
    for copy in ahead:
        copy.start()
    cw_ref[...] = cel_ref[...] * mask_ref[...].astype(F32)
    sum_ref[...] = jnp.zeros_like(sum_ref)
    pass_ref[...] = pass_in[...]
    propagate(speed_of(at_ref), UPWARD, -1, e_ref, cw_ref, table_ref, e2_ref, sum_ref)
    for copy in ahead:
        copy.wait()


def downward_kernel(at_ref, e_ref, cel_ref, mask_ref, sum_in, e2_ref, sum_ref, cw_ref, table_ref):
    cw_ref[...] = cel_ref[...] * mask_ref[...].astype(F32)
    sum_ref[...] = sum_in[...]
    propagate(speed_of(at_ref), DOWNWARD, 1, e_ref, cw_ref, table_ref, e2_ref, sum_ref)


def add_halo(speed, odd, dirs_ref, near_ref, far_ref, halos_ref, cel_ref, mask_ref, up_ref, down_ref, sum_ref):
    halos_ref[1 - odd] = near_ref[...]
    halos_ref[odd] = far_ref[...]
    sub = lax.broadcasted_iota(jnp.int32, (HALF, LANES), 0)
    lane = lax.broadcasted_iota(jnp.int32, (HALF, LANES), 1)
    zero = jnp.zeros((HALF, LANES), F32)
    for side, e2_ref, row, inside in ((0, down_ref, 0, 1), (1, up_ref, ROWS - 1, ROWS - 2)):
        ax, ay = speed * dirs_ref[2 * side, 0:HALF, :], speed * dirs_ref[2 * side + 1, 0:HALF, :]
        first = [ax * halos_ref[side, pl.ds(j * NDIR, HALF), :] for j in range(LTILES)]
        flux = [
            first[j] * (cel_ref[row : row + 1, lane_tile(j)] * mask_ref[row : row + 1, lane_tile(j)].astype(F32))
            for j in range(LTILES)
        ]
        right = [pltpu.roll(f, 1, 1) for f in flux]
        left = [pltpu.roll(f, LANES - 1, 1) for f in flux]
        for j in range(LTILES):
            r = jnp.where(lane == 0, right[j - 1] if j > 0 else zero, right[j])
            l = jnp.where(lane == LANES - 1, left[j + 1] if j + 1 < LTILES else zero, left[j])
            shifted = jnp.where(sub < QUARTER, r, l)
            outer = first[j] - (ax + ay) * flux[j] + ax * halos_ref[side, pl.ds(j * NDIR + HALF, HALF), :] + ay * shifted
            inner = ax * flux[j]
            for at, part in ((row, outer), (inside, inner)):
                for b in range(0, HALF - 2, 8):
                    cut = pl.ds(b * ROWS + at, 8, stride=ROWS)
                    e2_ref[j, cut, :] = e2_ref[j, cut, :] + part[b : b + 8]
                for b in range(HALF - 2, HALF):
                    e2_ref[j, b * ROWS + at : b * ROWS + at + 1, :] += part[b : b + 1]
                if sum_ref is not None:
                    wet = mask_ref[at : at + 1, lane_tile(j)].astype(F32)
                    sum_ref[j, at : at + 1, :] += wet * jnp.sum(part, axis=0, keepdims=True)


def rim_kernel(
    at_ref, dirs_ref, up_in, down_in, sum_in, near_ref, far_ref, cel_ref, mask_ref,
    up_ref, down_ref, sum_ref, halos_ref,
):
    del up_in, down_in
    for j in range(LTILES):
        sum_ref[j] = sum_in[j] * mask_ref[:, lane_tile(j)].astype(F32)
    add_halo(
        speed_of(at_ref), at_ref[0] & 1, dirs_ref, near_ref, far_ref, halos_ref, cel_ref, mask_ref, up_ref, down_ref, sum_ref
    )


def grow(j, speed, up_ref, down_ref, mask_ref, turn_ref, wind_ref, angle_ref, grown_ref):
    cols = pl.ds(pl.multiple_of(j * LANES, LANES), LANES)
    wet = mask_ref[:, cols].astype(F32)
    turn = turn_ref[:, cols] * speed
    wind = wind_ref[:, cols]
    angle = angle_ref[:, cols]
    stay = wet * (1.0 - jnp.abs(turn))
    from_low = wet * jnp.maximum(turn, 0.0)
    from_high = wet * jnp.maximum(-turn, 0.0)
    cosine = jnp.cos(angle)
    sine = jnp.sin(angle)
    gain = (0.3 * speed) * wind
    force = wet * 0.05 * wind * wind

    def load(k):
        k = k % NDIR
        ref, i = (up_ref, k - QUARTER) if k in UPWARD else (down_ref, DOWNWARD.index(k))
        return ref[j, pl.ds(i * ROWS, ROWS), :]

    low, here = load(NDIR - 1), load(0)
    for k in range(NDIR):
        high = load(k + 1)
        refracted = here * stay + low * from_low + high * from_high
        s = jnp.maximum(cosine * COS[k] + sine * SIN[k], 0.0)
        s = s * s
        grown_ref[j, pl.ds(k * STEP, ROWS), :] = refracted * (1.0 + gain * s) + force * s
        low, here = here, high


def grow_kernel(
    at_ref, picked_hbm, up_ref, down_ref, sum_ref, mask_ref, turn_ref, wind_ref, angle_ref,
    out_ref, grown_ref, send_ref, picked_ref, to_ref, sems,
):
    speed = speed_of(at_ref)
    fetch = pltpu.make_async_copy(picked_hbm, picked_ref, sems.at[1])
    fetch.start()

    def invert(g, carry):
        for d in range(8):
            to_ref[picked_ref[g * 8 + d]] = g * 8 + d
        return carry

    rows_ref = send_ref.reshape(DEVICES * SLOT, LANES)

    def tiles(j, carry):
        grow(j, speed, up_ref, down_ref, mask_ref, turn_ref, wind_ref, angle_ref, grown_ref)
        grown_ref[j, pl.ds(NDIR * STEP, ROWS), :] = sum_ref[j]

        @pl.when(j == 0)
        def _():
            fetch.wait()
            lax.fori_loop(0, DEVICES // 8, invert, 0)

        def pack(g, carry):
            for r in range(8):
                row = g * 8 + r
                at = (j * ROWS + row) * SLOT
                for b in (0, 8, 16, 24, SLOT - 8):
                    rows_ref[pl.ds(at + b, 8), :] = grown_ref[j, pl.ds(b * STEP + row, 8, stride=STEP), :]
                to = to_ref[row * LTILES + j] * SLOT
                pltpu.make_async_copy(send_ref.at[pl.ds(at, SLOT)], out_ref.at[pl.ds(to, SLOT)], sems.at[0]).start()
            return carry

        lax.fori_loop(0, ROWS // 8, pack, 0)
        return carry

    lax.fori_loop(0, LTILES, tiles, 0)
    pltpu.make_async_copy(send_ref, out_ref, sems.at[0]).wait()


def again_kernel(
    at_ref, dirs_ref, e_hbm, near_ref, far_ref, cel_ref, mask_ref, turn_ref, wind_ref, angle_ref,
    grown_hbm, grown_ref, up_e, down_e, up_ref, down_ref, sum_ref, halos_ref, cw_ref, table_ref, sems,
):
    copies = [
        pltpu.make_async_copy(e_hbm.at[pl.ds(QUARTER, HALF)], up_e, sems.at[0]),
        pltpu.make_async_copy(e_hbm.at[pl.ds(0, QUARTER)], down_e.at[pl.ds(0, QUARTER)], sems.at[1]),
        pltpu.make_async_copy(e_hbm.at[pl.ds(3 * QUARTER, QUARTER)], down_e.at[pl.ds(QUARTER, QUARTER)], sems.at[2]),
    ]
    for copy in copies:
        copy.start()
    speed = speed_of(at_ref)
    cw_ref[...] = cel_ref[...] * mask_ref[...].astype(F32)
    sum_ref[...] = jnp.zeros_like(sum_ref)
    for copy in copies:
        copy.wait()
    propagate(speed, UPWARD, -1, up_e, cw_ref, table_ref, up_ref, sum_ref)
    propagate(speed, DOWNWARD, 1, down_e, cw_ref, table_ref, down_ref, sum_ref)
    add_halo(speed, at_ref[0] & 1, dirs_ref, near_ref, far_ref, halos_ref, cel_ref, mask_ref, up_ref, down_ref, None)

    def tiles(j, carry):
        grow(j, speed, up_ref, down_ref, mask_ref, turn_ref, wind_ref, angle_ref, grown_ref)
        return carry

    lax.fori_loop(0, LTILES, tiles, 0)
    store = pltpu.make_async_copy(grown_ref, grown_hbm, sems.at[0])
    store.start()
    store.wait()


def home_kernel(at_ref, grown_ref, mine_ref, other_ref, out_ref, stage_ref, scale_ref, sems):
    speed = speed_of(at_ref)
    for j in range(LTILES):
        mean = (mine_ref[j] + other_ref[j]) * (1.0 / NBINS)
        scale_ref[j] = 1.0 / (1.0 + (2.0 * speed * speed) * mean / (1.0 + mean))
    copies = []
    for part in range(4):
        for j in range(LTILES):
            scale = scale_ref[j]
            for k in range(part * QUARTER, (part + 1) * QUARTER):
                stage_ref[k, :, lane_tile(j)] = grown_ref[j, pl.ds(k * STEP, ROWS), :] * scale
        cut = pl.ds(part * QUARTER, QUARTER)
        copies.append(pltpu.make_async_copy(stage_ref.at[cut], out_ref.at[cut], sems.at[part]))
        copies[-1].start()
    for copy in copies:
        copy.wait()


def owner_kernel(slots_ref, factor_ref, got_ref, out_ref, stage_ref, scale_ref, sems):
    copies = []
    for b in range(OWN):
        sums = got_ref[pl.ds(b * SLOT + NDIR, NFREQ, stride=OWN * SLOT), :]
        mean = jnp.sum(sums, axis=0, keepdims=True) * (1.0 / NBINS)
        scale_ref[b] = 1.0 / (1.0 + factor_ref[...] * mean / (1.0 + mean))
    for b in range(OWN):
        for s in range(NFREQ):
            stage_ref[b, pl.ds(s * NDIR, NDIR), :] = (
                got_ref[pl.ds((s * OWN + b) * SLOT, NDIR), :] * scale_ref[b, s : s + 1, :]
            )
        copies.append(pltpu.make_async_copy(stage_ref.at[b], out_ref.at[slots_ref[b]], sems.at[b]))
        copies[-1].start()
    for copy in copies:
        copy.wait()


def shards(spectrum, land_mask, celerity, turning, wind_speed, wind_dir, tile_order):
    band = lax.axis_index("space")
    me = lax.axis_index(("spec", "space"))
    at = me.astype(jnp.int32).reshape(1)
    space_count = lax.axis_size("space")
    spec_count = lax.axis_size("spec")
    shape = jax.ShapeDtypeStruct

    planes = shape((HALF, ROWS, COLS), F32)
    halves = shape((LTILES, HALF * ROWS, LANES), F32)
    rims = shape((LTILES * NDIR, LANES), F32)
    summed = shape((LTILES, ROWS, LANES), F32)
    near_rim, far_rim, up_e = pl.pallas_call(
        edge_kernel,
        out_shape=(rims, rims, planes),
        in_specs=[SMEM_SPEC] + [HBM_SPEC] * 3,
        out_specs=(VMEM_SPEC,) * 3,
        scratch_shapes=[
            pltpu.VMEM((2, HALF, 8, COLS), F32),
            pltpu.VMEM((2, 8, COLS), F32),
            pltpu.VMEM((2, 8, COLS), jnp.int32),
            pltpu.VMEM((2, LTILES * NDIR, LANES), F32),
            pltpu.SemaphoreType.DMA((8,)),
        ],
        compiler_params=PARAMS,
        name="edges",
    )(at, in_hbm(spectrum), in_hbm(celerity), in_hbm(land_mask))
    within = [(i, i ^ 1) for i in range(space_count)]
    across = [(i, i + 1) for i in range(1, space_count - 1, 2)]
    across = across + [(b, a) for a, b in across]
    far = lax.ppermute(far_rim, "space", across)
    scratch = [pltpu.VMEM((ROWS, COLS), F32), pltpu.SMEM((2, HALF), F32)]
    up_e2, sums, near_rim, down_e = pl.pallas_call(
        upward_kernel,
        out_shape=(halves, summed, rims, planes),
        in_specs=[SMEM_SPEC, HBM_SPEC] + [VMEM_SPEC] * 4,
        out_specs=(VMEM_SPEC,) * 4,
        scratch_shapes=scratch + [pltpu.SemaphoreType.DMA((2,))],
        compiler_params=PARAMS,
        name="upward",
    )(at, in_hbm(spectrum), up_e, celerity, land_mask, near_rim)
    near = lax.ppermute(near_rim, "space", within)
    down_e2, sums = pl.pallas_call(
        downward_kernel,
        out_shape=(halves, summed),
        in_specs=[SMEM_SPEC] + [VMEM_SPEC] * 4,
        out_specs=(VMEM_SPEC,) * 2,
        scratch_shapes=scratch,
        compiler_params=PARAMS,
        name="downward",
    )(at, down_e, celerity, land_mask, sums)

    per_band = ROWS * LTILES
    order = tile_order.reshape(DEVICES, OWN)
    picked = jnp.sum(jnp.where(order // per_band == band, order % per_band, 0), axis=1).astype(jnp.int32)
    own = lax.dynamic_slice_in_dim(order, me, 1, 0).reshape(OWN) // per_band
    slots = jnp.sum(
        jnp.where(own[None, :] == jnp.arange(OWN)[:, None], jnp.arange(OWN)[None, :], 0), axis=1
    ).astype(jnp.int32)

    table = np.zeros((4, EDGE_PAD, LANES), np.float32)
    for i, dirs in enumerate((DOWNWARD, UPWARD)):
        table[2 * i, :HALF] = np.array([ABS_X[k] for k in dirs], np.float32)[:, None]
        table[2 * i + 1, :HALF] = np.array([ABS_Y[k] for k in dirs], np.float32)[:, None]
    table = jnp.asarray(table)
    up_e2, down_e2, sums = pl.pallas_call(
        rim_kernel,
        out_shape=(halves, halves, summed),
        in_specs=[SMEM_SPEC] + [VMEM_SPEC] * 8,
        out_specs=(VMEM_SPEC,) * 3,
        scratch_shapes=[pltpu.VMEM((2, LTILES * NDIR, LANES), F32)],
        input_output_aliases={2: 0, 3: 1},
        compiler_params=PARAMS,
        name="rims",
    )(at, table, up_e2, down_e2, sums, near, far, celerity, land_mask)

    send = pl.pallas_call(
        grow_kernel,
        out_shape=pltpu.HBM((DEVICES * SLOT, 1, LANES), F32),
        in_specs=[SMEM_SPEC, ANY_SPEC] + [VMEM_SPEC] * 7,
        out_specs=HBM_SPEC,
        scratch_shapes=[
            pltpu.VMEM((LTILES, GROWN, LANES), F32),
            pltpu.VMEM((DEVICES * SLOT, 1, LANES), F32),
            pltpu.SMEM((DEVICES,), jnp.int32),
            pltpu.SMEM((DEVICES,), jnp.int32),
            pltpu.SemaphoreType.DMA((2,)),
        ],
        compiler_params=PARAMS,
        name="grow",
    )(at, picked, up_e2, down_e2, sums, land_mask, turning, wind_speed, wind_dir)

    def over_spec(x, masks):
        return [lax.ppermute(x, "spec", [(i, i ^ n) for i in range(spec_count)]) for n in masks]

    (pair,) = over_spec(sums, (4,))
    send, pair = lax.optimization_barrier((send, pair))
    twos = sums + pair
    got = lax.all_to_all(
        send.reshape(DEVICES, SLOT, 1, LANES), ("spec", "space"), split_axis=0, concat_axis=0, tiled=True
    ).reshape(DEVICES * SLOT, LANES)
    fours = over_spec(twos, (3, 12, 15))

    near, far, pair = lax.optimization_barrier((near, far, pair))
    grown = pl.pallas_call(
        again_kernel,
        out_shape=pltpu.HBM((LTILES, GROWN, LANES), F32),
        in_specs=[SMEM_SPEC, VMEM_SPEC, HBM_SPEC] + [VMEM_SPEC] * 7,
        out_specs=HBM_SPEC,
        scratch_shapes=[pltpu.VMEM((LTILES, GROWN, LANES), F32)]
        + [pltpu.VMEM((HALF, ROWS, COLS), F32)] * 2
        + [pltpu.VMEM((LTILES, HALF * ROWS, LANES), F32)] * 2
        + [pltpu.VMEM((LTILES, ROWS, LANES), F32), pltpu.VMEM((2, LTILES * NDIR, LANES), F32)]
        + scratch
        + [pltpu.SemaphoreType.DMA((3,))],
        compiler_params=PARAMS,
        name="again",
    )(at, table, in_hbm(spectrum), near, far, celerity, land_mask, turning, wind_speed, wind_dir)

    fours[0], grown = lax.optimization_barrier((fours[0], grown))
    eights = twos + fours[0] + fours[1] + fours[2]
    (other,) = over_spec(eights, (1,))

    factor = jnp.asarray(np.repeat(2.0 * SPEED[:, None] * SPEED[:, None], LANES, axis=1), F32)
    tile_spectra = pl.pallas_call(
        owner_kernel,
        out_shape=shape((OWN, NBINS, LANES), F32),
        in_specs=[SMEM_SPEC] + [VMEM_SPEC] * 2,
        out_specs=HBM_SPEC,
        scratch_shapes=[
            pltpu.VMEM((OWN, NBINS, LANES), F32),
            pltpu.VMEM((OWN, NFREQ, LANES), F32),
            pltpu.SemaphoreType.DMA((OWN,)),
        ],
        compiler_params=PARAMS,
        name="owned",
    )(slots, factor, got)

    other, tile_spectra = lax.optimization_barrier((other, tile_spectra))
    spectrum_next = pl.pallas_call(
        home_kernel,
        out_shape=shape((NDIR, ROWS, COLS), F32),
        in_specs=[SMEM_SPEC] + [VMEM_SPEC] * 3,
        out_specs=HBM_SPEC,
        scratch_shapes=[
            pltpu.VMEM((NDIR, ROWS, COLS), F32),
            pltpu.VMEM((LTILES, ROWS, LANES), F32),
            pltpu.SemaphoreType.DMA((4,)),
        ],
        compiler_params=PARAMS,
        name="home",
    )(at, grown, eights, other)
    return spectrum_next, tile_spectra


def solution(mesh):
    return jax.shard_map(
        shards,
        mesh=mesh,
        in_specs=(
            P("spec", "space", None),
            P("space", None),
            P("space", None),
            P("space", None),
            P("space", None),
            P("space", None),
            P(),
        ),
        out_specs=(P("spec", "space", None), P(("spec", "space"), None, None)),
        check_vma=False,
    )
```

```python
import math

import jax
import jax.numpy as jnp
import numpy as np
from jax import lax
from jax.experimental import pallas as pl
from jax.experimental.pallas import tpu as pltpu
from jax.sharding import PartitionSpec as P

NDIR = 36
NFREQ = 16
NBINS = NDIR * NFREQ
ROWS = 32
COLS = 512
LANES = 128
LTILES = COLS // LANES
STILES = ROWS // 8
DEVICES = 128
OWN = 8
SLOT = NDIR + 1
QUARTER = NDIR // 4
HALF = NDIR // 2
STEP = ROWS + 1
GROWN = (SLOT * STEP + 7) // 8 * 8
EDGE_PAD = 24
PIECE = 3
FREQ_RATIO = 1.1
COURANT = 0.45

THETA = [2.0 * math.pi * (k + 0.5) / NDIR for k in range(NDIR)]
COS = [float(np.float32(math.cos(t))) for t in THETA]
SIN = [float(np.float32(math.sin(t))) for t in THETA]
ABS_X = [float(np.float32(COURANT * abs(math.cos(t)))) for t in THETA]
ABS_Y = [float(np.float32(COURANT * abs(math.sin(t)))) for t in THETA]
SPEED = np.array([FREQ_RATIO ** (-i) for i in range(NFREQ)], np.float32)
DOWNWARD = list(range(QUARTER)) + list(range(3 * QUARTER, NDIR))
UPWARD = list(range(QUARTER, 3 * QUARTER))

SMEM_SPEC = pl.BlockSpec(memory_space=pltpu.SMEM)
VMEM_SPEC = pl.BlockSpec(memory_space=pltpu.VMEM)
HBM_SPEC = pl.BlockSpec(memory_space=pltpu.HBM)
ANY_SPEC = pl.BlockSpec(memory_space=pl.ANY)
PARAMS = pltpu.CompilerParams(vmem_limit_bytes=16 * 1024 * 1024)
F32 = jnp.float32


def speed_of(at_ref):
    index = at_ref[0] >> 3
    speed = jnp.float32(1.0)
    for bit in (1, 2, 4, 8):
        speed = speed * jnp.where((index & bit) != 0, jnp.float32(FREQ_RATIO ** (-bit)), jnp.float32(1.0))
    return speed


def in_hbm(x):
    return pltpu.with_memory_space_constraint(x, pltpu.HBM)


def lane_tile(j):
    return pl.ds(j * LANES, LANES)


def iotas():
    return (lax.broadcasted_iota(jnp.int32, (8, LANES), 0), lax.broadcasted_iota(jnp.int32, (8, LANES), 1))


def column_shift(tiles, sign, lane):
    edge = 0 if sign > 0 else LANES - 1
    turned = [pltpu.roll(t, 1 if sign > 0 else LANES - 1, 1) for t in tiles]
    zero = jnp.zeros_like(tiles[0])
    out = []
    for j in range(len(tiles)):
        at = j - sign
        out.append(jnp.where(lane == edge, turned[at] if 0 <= at < len(tiles) else zero, turned[j]))
    return out


def row_shift(tiles, sign, sub):
    edge = 0 if sign > 0 else 7
    turned = [pltpu.roll(t, 1 if sign > 0 else 7, 0) for t in tiles]
    zero = jnp.zeros_like(tiles[0])
    out = []
    for i in range(len(tiles)):
        at = i - sign
        out.append(jnp.where(sub == edge, turned[at] if 0 <= at < len(tiles) else zero, turned[i]))
    return out


def advance(energy, flux, ax, ay, sx, sy, sub, lane):
    n = len(energy)
    by_col = [column_shift(flux[i], sy, lane) for i in range(n)]
    total = ax + ay
    out = [[None] * LTILES for _ in range(n)]
    for j in range(LTILES):
        by_row = row_shift([flux[i][j] for i in range(n)], sx, sub)
        for i in range(n):
            out[i][j] = energy[i][j] - total * flux[i][j] + ax * by_row[i] + ay * by_col[i][j]
    return out


def edge_kernel(at_ref, e_ref, cel_ref, mask_ref, near_ref, far_ref, up_e_ref, edge_e, cels, masks, rim_ref, sems):
    copies = [
        pltpu.make_async_copy(e_ref.at[pl.ds(0, QUARTER), pl.ds(ROWS - 8, 8), :], edge_e.at[0, pl.ds(0, QUARTER)], sems.at[0]),
        pltpu.make_async_copy(
            e_ref.at[pl.ds(3 * QUARTER, QUARTER), pl.ds(ROWS - 8, 8), :], edge_e.at[0, pl.ds(QUARTER, QUARTER)], sems.at[1]
        ),
        pltpu.make_async_copy(e_ref.at[pl.ds(QUARTER, HALF), pl.ds(0, 8), :], edge_e.at[1], sems.at[2]),
        pltpu.make_async_copy(cel_ref.at[pl.ds(ROWS - 8, 8), :], cels.at[0], sems.at[3]),
        pltpu.make_async_copy(mask_ref.at[pl.ds(ROWS - 8, 8), :], masks.at[0], sems.at[4]),
        pltpu.make_async_copy(cel_ref.at[pl.ds(0, 8), :], cels.at[1], sems.at[5]),
        pltpu.make_async_copy(mask_ref.at[pl.ds(0, 8), :], masks.at[1], sems.at[6]),
    ]
    for n in (3, 4, 0, 1, 5, 6, 2):
        copies[n].start()
    ahead = pltpu.make_async_copy(e_ref.at[pl.ds(QUARTER, HALF)], up_e_ref, sems.at[7])
    ahead.start()
    sub, lane = iotas()
    speed = speed_of(at_ref)
    odd = at_ref[0] & 1
    for side, dirs, row, sx in ((0, DOWNWARD, 7, 1), (1, UPWARD, 0, -1)):
        for n in ((0, 1, 3, 4), (2, 5, 6))[side]:
            copies[n].wait()
        cw = [cels[side, :, lane_tile(j)] * masks[side, :, lane_tile(j)].astype(F32) for j in range(LTILES)]
        out = odd if side == 0 else 1 - odd
        for i, k in enumerate(dirs):
            ax, ay = speed * ABS_X[k], speed * ABS_Y[k]
            energy = [edge_e[side, i, :, lane_tile(j)] for j in range(LTILES)]
            flux = [cw[j] * energy[j] for j in range(LTILES)]
            after = advance([energy], [flux], ax, ay, sx, 1 if SIN[k] > 0 else -1, sub, lane)[0]
            for j in range(LTILES):
                rim_ref[out, pl.ds(j * NDIR + i, 1), :] = flux[j][row : row + 1]
                rim_ref[out, pl.ds(j * NDIR + HALF + i, 1), :] = (cw[j] * after[j])[row : row + 1]
    near_ref[...] = rim_ref[0]
    far_ref[...] = rim_ref[1]
    ahead.wait()


def propagate(speed, dirs, sx, e_ref, cw_ref, table_ref, e2_ref, sum_ref):
    sub, lane = iotas()
    for i, k in enumerate(dirs):
        table_ref[0, i] = speed * ABS_X[k]
        table_ref[1, i] = speed * ABS_Y[k]

    for half, sy in ((0, 1), (1, -1)):

        def body(piece, carry):
            total = None
            for d in range(PIECE):
                i = half * QUARTER + piece * PIECE + d
                ax, ay = table_ref[0, i], table_ref[1, i]
                cw = [[cw_ref[pl.ds(8 * r, 8), lane_tile(j)] for j in range(LTILES)] for r in range(STILES)]
                energy = [[e_ref[i, pl.ds(8 * r, 8), lane_tile(j)] for j in range(LTILES)] for r in range(STILES)]
                for _ in range(2):
                    flux = [[cw[r][j] * energy[r][j] for j in range(LTILES)] for r in range(STILES)]
                    energy = advance(energy, flux, ax, ay, sx, sy, sub, lane)
                for r in range(STILES):
                    for j in range(LTILES):
                        e2_ref[j, pl.ds(pl.multiple_of(i * ROWS, 8) + 8 * r, 8), :] = energy[r][j]
                total = energy if total is None else [[t + e for t, e in zip(x, y)] for x, y in zip(total, energy)]
            for r in range(STILES):
                for j in range(LTILES):
                    sum_ref[j, pl.ds(8 * r, 8), :] += total[r][j]
            return carry

        lax.fori_loop(0, QUARTER // PIECE, body, 0)


def upward_kernel(
    at_ref, e_hbm, e_ref, cel_ref, mask_ref, pass_in, e2_ref, sum_ref, pass_ref, down_e_ref, cw_ref, table_ref, sems
):
    ahead = [
        pltpu.make_async_copy(e_hbm.at[pl.ds(0, QUARTER)], down_e_ref.at[pl.ds(0, QUARTER)], sems.at[0]),
        pltpu.make_async_copy(e_hbm.at[pl.ds(3 * QUARTER, QUARTER)], down_e_ref.at[pl.ds(QUARTER, QUARTER)], sems.at[1]),
    ]
    for copy in ahead:
        copy.start()
    cw_ref[...] = cel_ref[...] * mask_ref[...].astype(F32)
    sum_ref[...] = jnp.zeros_like(sum_ref)
    pass_ref[...] = pass_in[...]
    propagate(speed_of(at_ref), UPWARD, -1, e_ref, cw_ref, table_ref, e2_ref, sum_ref)
    for copy in ahead:
        copy.wait()


def downward_kernel(at_ref, e_ref, cel_ref, mask_ref, sum_in, e2_ref, sum_ref, cw_ref, table_ref):
    cw_ref[...] = cel_ref[...] * mask_ref[...].astype(F32)
    sum_ref[...] = sum_in[...]
    propagate(speed_of(at_ref), DOWNWARD, 1, e_ref, cw_ref, table_ref, e2_ref, sum_ref)


def add_halo(speed, odd, dirs_ref, near_ref, far_ref, halos_ref, cel_ref, mask_ref, up_ref, down_ref, sum_ref):
    halos_ref[1 - odd] = near_ref[...]
    halos_ref[odd] = far_ref[...]
    sub = lax.broadcasted_iota(jnp.int32, (HALF, LANES), 0)
    lane = lax.broadcasted_iota(jnp.int32, (HALF, LANES), 1)
    zero = jnp.zeros((HALF, LANES), F32)
    for side, e2_ref, row, inside in ((0, down_ref, 0, 1), (1, up_ref, ROWS - 1, ROWS - 2)):
        ax, ay = speed * dirs_ref[2 * side, 0:HALF, :], speed * dirs_ref[2 * side + 1, 0:HALF, :]
        first = [ax * halos_ref[side, pl.ds(j * NDIR, HALF), :] for j in range(LTILES)]
        flux = [
            first[j] * (cel_ref[row : row + 1, lane_tile(j)] * mask_ref[row : row + 1, lane_tile(j)].astype(F32))
            for j in range(LTILES)
        ]
        right = [pltpu.roll(f, 1, 1) for f in flux]
        left = [pltpu.roll(f, LANES - 1, 1) for f in flux]
        for j in range(LTILES):
            r = jnp.where(lane == 0, right[j - 1] if j > 0 else zero, right[j])
            l = jnp.where(lane == LANES - 1, left[j + 1] if j + 1 < LTILES else zero, left[j])
            shifted = jnp.where(sub < QUARTER, r, l)
            outer = first[j] - (ax + ay) * flux[j] + ax * halos_ref[side, pl.ds(j * NDIR + HALF, HALF), :] + ay * shifted
            inner = ax * flux[j]
            for at, part in ((row, outer), (inside, inner)):
                for b in range(0, HALF - 2, 8):
                    cut = pl.ds(b * ROWS + at, 8, stride=ROWS)
                    e2_ref[j, cut, :] = e2_ref[j, cut, :] + part[b : b + 8]
                for b in range(HALF - 2, HALF):
                    e2_ref[j, b * ROWS + at : b * ROWS + at + 1, :] += part[b : b + 1]
                if sum_ref is not None:
                    wet = mask_ref[at : at + 1, lane_tile(j)].astype(F32)
                    sum_ref[j, at : at + 1, :] += wet * jnp.sum(part, axis=0, keepdims=True)


def rim_kernel(
    at_ref, dirs_ref, up_in, down_in, sum_in, near_ref, far_ref, cel_ref, mask_ref,
    up_ref, down_ref, sum_ref, halos_ref,
):
    del up_in, down_in
    for j in range(LTILES):
        sum_ref[j] = sum_in[j] * mask_ref[:, lane_tile(j)].astype(F32)
    add_halo(
        speed_of(at_ref), at_ref[0] & 1, dirs_ref, near_ref, far_ref, halos_ref, cel_ref, mask_ref, up_ref, down_ref, sum_ref
    )


def grow(j, speed, up_ref, down_ref, mask_ref, turn_ref, wind_ref, angle_ref, grown_ref):
    cols = pl.ds(pl.multiple_of(j * LANES, LANES), LANES)
    wet = mask_ref[:, cols].astype(F32)
    turn = turn_ref[:, cols] * speed
    wind = wind_ref[:, cols]
    angle = angle_ref[:, cols]
    stay = wet * (1.0 - jnp.abs(turn))
    from_low = wet * jnp.maximum(turn, 0.0)
    from_high = wet * jnp.maximum(-turn, 0.0)
    cosine = jnp.cos(angle)
    sine = jnp.sin(angle)
    gain = (0.3 * speed) * wind
    force = wet * 0.05 * wind * wind

    def load(k):
        k = k % NDIR
        ref, i = (up_ref, k - QUARTER) if k in UPWARD else (down_ref, DOWNWARD.index(k))
        return ref[j, pl.ds(i * ROWS, ROWS), :]

    low, here = load(NDIR - 1), load(0)
    for k in range(NDIR):
        high = load(k + 1)
        refracted = here * stay + low * from_low + high * from_high
        s = jnp.maximum(cosine * COS[k] + sine * SIN[k], 0.0)
        s = s * s
        grown_ref[j, pl.ds(k * STEP, ROWS), :] = refracted * (1.0 + gain * s) + force * s
        low, here = here, high


def grow_kernel(
    at_ref, picked_hbm, up_ref, down_ref, sum_ref, mask_ref, turn_ref, wind_ref, angle_ref,
    out_ref, grown_ref, send_ref, picked_ref, to_ref, sems,
):
    speed = speed_of(at_ref)
    fetch = pltpu.make_async_copy(picked_hbm, picked_ref, sems.at[1])
    fetch.start()

    def invert(g, carry):
        for d in range(8):
            to_ref[picked_ref[g * 8 + d]] = g * 8 + d
        return carry

    rows_ref = send_ref.reshape(DEVICES * SLOT, LANES)

    def tiles(j, carry):
        grow(j, speed, up_ref, down_ref, mask_ref, turn_ref, wind_ref, angle_ref, grown_ref)
        grown_ref[j, pl.ds(NDIR * STEP, ROWS), :] = sum_ref[j]

        @pl.when(j == 0)
        def _():
            fetch.wait()
            lax.fori_loop(0, DEVICES // 8, invert, 0)

        def pack(g, carry):
            for r in range(8):
                row = g * 8 + r
                at = (j * ROWS + row) * SLOT
                for b in (0, 8, 16, 24, SLOT - 8):
                    rows_ref[pl.ds(at + b, 8), :] = grown_ref[j, pl.ds(b * STEP + row, 8, stride=STEP), :]
                to = to_ref[row * LTILES + j] * SLOT
                pltpu.make_async_copy(send_ref.at[pl.ds(at, SLOT)], out_ref.at[pl.ds(to, SLOT)], sems.at[0]).start()
            return carry

        lax.fori_loop(0, ROWS // 8, pack, 0)
        return carry

    lax.fori_loop(0, LTILES, tiles, 0)
    pltpu.make_async_copy(send_ref, out_ref, sems.at[0]).wait()


def again_kernel(
    at_ref, dirs_ref, e_hbm, near_ref, far_ref, cel_ref, mask_ref, turn_ref, wind_ref, angle_ref,
    grown_hbm, grown_ref, up_e, down_e, up_ref, down_ref, sum_ref, halos_ref, cw_ref, table_ref, sems,
):
    copies = [
        pltpu.make_async_copy(e_hbm.at[pl.ds(QUARTER, HALF)], up_e, sems.at[0]),
        pltpu.make_async_copy(e_hbm.at[pl.ds(0, QUARTER)], down_e.at[pl.ds(0, QUARTER)], sems.at[1]),
        pltpu.make_async_copy(e_hbm.at[pl.ds(3 * QUARTER, QUARTER)], down_e.at[pl.ds(QUARTER, QUARTER)], sems.at[2]),
    ]
    for copy in copies:
        copy.start()
    speed = speed_of(at_ref)
    cw_ref[...] = cel_ref[...] * mask_ref[...].astype(F32)
    sum_ref[...] = jnp.zeros_like(sum_ref)
    for copy in copies:
        copy.wait()
    propagate(speed, UPWARD, -1, up_e, cw_ref, table_ref, up_ref, sum_ref)
    propagate(speed, DOWNWARD, 1, down_e, cw_ref, table_ref, down_ref, sum_ref)
    add_halo(speed, at_ref[0] & 1, dirs_ref, near_ref, far_ref, halos_ref, cel_ref, mask_ref, up_ref, down_ref, None)

    def tiles(j, carry):
        grow(j, speed, up_ref, down_ref, mask_ref, turn_ref, wind_ref, angle_ref, grown_ref)
        return carry

    lax.fori_loop(0, LTILES, tiles, 0)
    store = pltpu.make_async_copy(grown_ref, grown_hbm, sems.at[0])
    store.start()
    store.wait()


def home_kernel(at_ref, grown_ref, mine_ref, other_ref, out_ref, stage_ref, scale_ref, sems):
    speed = speed_of(at_ref)
    for j in range(LTILES):
        mean = (mine_ref[j] + other_ref[j]) * (1.0 / NBINS)
        scale_ref[j] = 1.0 / (1.0 + (2.0 * speed * speed) * mean / (1.0 + mean))
    copies = []
    for part in range(4):
        for j in range(LTILES):
            scale = scale_ref[j]
            for k in range(part * QUARTER, (part + 1) * QUARTER):
                stage_ref[k, :, lane_tile(j)] = grown_ref[j, pl.ds(k * STEP, ROWS), :] * scale
        cut = pl.ds(part * QUARTER, QUARTER)
        copies.append(pltpu.make_async_copy(stage_ref.at[cut], out_ref.at[cut], sems.at[part]))
        copies[-1].start()
    for copy in copies:
        copy.wait()


def owner_kernel(slots_ref, factor_ref, got_ref, out_ref, stage_ref, scale_ref, sems):
    copies = []
    for b in range(OWN):
        sums = got_ref[pl.ds(b * SLOT + NDIR, NFREQ, stride=OWN * SLOT), :]
        mean = jnp.sum(sums, axis=0, keepdims=True) * (1.0 / NBINS)
        scale_ref[b] = 1.0 / (1.0 + factor_ref[...] * mean / (1.0 + mean))
    for b in range(OWN):
        for s in range(NFREQ):
            stage_ref[b, pl.ds(s * NDIR, NDIR), :] = (
                got_ref[pl.ds((s * OWN + b) * SLOT, NDIR), :] * scale_ref[b, s : s + 1, :]
            )
        copies.append(pltpu.make_async_copy(stage_ref.at[b], out_ref.at[slots_ref[b]], sems.at[b]))
        copies[-1].start()
    for copy in copies:
        copy.wait()


def shards(spectrum, land_mask, celerity, turning, wind_speed, wind_dir, tile_order):
    band = lax.axis_index("space")
    me = lax.axis_index(("spec", "space"))
    at = me.astype(jnp.int32).reshape(1)
    space_count = lax.axis_size("space")
    spec_count = lax.axis_size("spec")
    shape = jax.ShapeDtypeStruct

    planes = shape((HALF, ROWS, COLS), F32)
    halves = shape((LTILES, HALF * ROWS, LANES), F32)
    rims = shape((LTILES * NDIR, LANES), F32)
    summed = shape((LTILES, ROWS, LANES), F32)
    near_rim, far_rim, up_e = pl.pallas_call(
        edge_kernel,
        out_shape=(rims, rims, planes),
        in_specs=[SMEM_SPEC] + [HBM_SPEC] * 3,
        out_specs=(VMEM_SPEC,) * 3,
        scratch_shapes=[
            pltpu.VMEM((2, HALF, 8, COLS), F32),
            pltpu.VMEM((2, 8, COLS), F32),
            pltpu.VMEM((2, 8, COLS), jnp.int32),
            pltpu.VMEM((2, LTILES * NDIR, LANES), F32),
            pltpu.SemaphoreType.DMA((8,)),
        ],
        compiler_params=PARAMS,
        name="edges",
    )(at, in_hbm(spectrum), in_hbm(celerity), in_hbm(land_mask))
    within = [(i, i ^ 1) for i in range(space_count)]
    across = [(i, i + 1) for i in range(1, space_count - 1, 2)]
    across = across + [(b, a) for a, b in across]
    far = lax.ppermute(far_rim, "space", across)
    scratch = [pltpu.VMEM((ROWS, COLS), F32), pltpu.SMEM((2, HALF), F32)]
    up_e2, sums, near_rim, down_e = pl.pallas_call(
        upward_kernel,
        out_shape=(halves, summed, rims, planes),
        in_specs=[SMEM_SPEC, HBM_SPEC] + [VMEM_SPEC] * 4,
        out_specs=(VMEM_SPEC,) * 4,
        scratch_shapes=scratch + [pltpu.SemaphoreType.DMA((2,))],
        compiler_params=PARAMS,
        name="upward",
    )(at, in_hbm(spectrum), up_e, celerity, land_mask, near_rim)
    near = lax.ppermute(near_rim, "space", within)
    down_e2, sums = pl.pallas_call(
        downward_kernel,
        out_shape=(halves, summed),
        in_specs=[SMEM_SPEC] + [VMEM_SPEC] * 4,
        out_specs=(VMEM_SPEC,) * 2,
        scratch_shapes=scratch,
        compiler_params=PARAMS,
        name="downward",
    )(at, down_e, celerity, land_mask, sums)

    per_band = ROWS * LTILES
    order = tile_order.reshape(DEVICES, OWN)
    picked = jnp.sum(jnp.where(order // per_band == band, order % per_band, 0), axis=1).astype(jnp.int32)
    own = lax.dynamic_slice_in_dim(order, me, 1, 0).reshape(OWN) // per_band
    slots = jnp.sum(
        jnp.where(own[None, :] == jnp.arange(OWN)[:, None], jnp.arange(OWN)[None, :], 0), axis=1
    ).astype(jnp.int32)

    table = np.zeros((4, EDGE_PAD, LANES), np.float32)
    for i, dirs in enumerate((DOWNWARD, UPWARD)):
        table[2 * i, :HALF] = np.array([ABS_X[k] for k in dirs], np.float32)[:, None]
        table[2 * i + 1, :HALF] = np.array([ABS_Y[k] for k in dirs], np.float32)[:, None]
    table = jnp.asarray(table)
    up_e2, down_e2, sums = pl.pallas_call(
        rim_kernel,
        out_shape=(halves, halves, summed),
        in_specs=[SMEM_SPEC] + [VMEM_SPEC] * 8,
        out_specs=(VMEM_SPEC,) * 3,
        scratch_shapes=[pltpu.VMEM((2, LTILES * NDIR, LANES), F32)],
        input_output_aliases={2: 0, 3: 1},
        compiler_params=PARAMS,
        name="rims",
    )(at, table, up_e2, down_e2, sums, near, far, celerity, land_mask)

    send = pl.pallas_call(
        grow_kernel,
        out_shape=pltpu.HBM((DEVICES * SLOT, 1, LANES), F32),
        in_specs=[SMEM_SPEC, ANY_SPEC] + [VMEM_SPEC] * 7,
        out_specs=HBM_SPEC,
        scratch_shapes=[
            pltpu.VMEM((LTILES, GROWN, LANES), F32),
            pltpu.VMEM((DEVICES * SLOT, 1, LANES), F32),
            pltpu.SMEM((DEVICES,), jnp.int32),
            pltpu.SMEM((DEVICES,), jnp.int32),
            pltpu.SemaphoreType.DMA((2,)),
        ],
        compiler_params=PARAMS,
        name="grow",
    )(at, picked, up_e2, down_e2, sums, land_mask, turning, wind_speed, wind_dir)

    def over_spec(x, masks):
        return [lax.ppermute(x, "spec", [(i, i ^ n) for i in range(spec_count)]) for n in masks]

    (pair,) = over_spec(sums, (4,))
    send, pair = lax.optimization_barrier((send, pair))
    twos = sums + pair
    got = lax.all_to_all(
        send.reshape(DEVICES, SLOT, 1, LANES), ("spec", "space"), split_axis=0, concat_axis=0, tiled=True
    ).reshape(DEVICES * SLOT, LANES)
    fours = over_spec(twos, (3, 12, 15))

    near, far, pair = lax.optimization_barrier((near, far, pair))
    grown = pl.pallas_call(
        again_kernel,
        out_shape=pltpu.HBM((LTILES, GROWN, LANES), F32),
        in_specs=[SMEM_SPEC, VMEM_SPEC, HBM_SPEC] + [VMEM_SPEC] * 7,
        out_specs=HBM_SPEC,
        scratch_shapes=[pltpu.VMEM((LTILES, GROWN, LANES), F32)]
        + [pltpu.VMEM((HALF, ROWS, COLS), F32)] * 2
        + [pltpu.VMEM((LTILES, HALF * ROWS, LANES), F32)] * 2
        + [pltpu.VMEM((LTILES, ROWS, LANES), F32), pltpu.VMEM((2, LTILES * NDIR, LANES), F32)]
        + scratch
        + [pltpu.SemaphoreType.DMA((3,))],
        compiler_params=PARAMS,
        name="again",
    )(at, table, in_hbm(spectrum), near, far, celerity, land_mask, turning, wind_speed, wind_dir)

    fours[0], grown = lax.optimization_barrier((fours[0], grown))
    eights = twos + fours[0] + fours[1] + fours[2]
    (other,) = over_spec(eights, (1,))

    factor = jnp.asarray(np.repeat(2.0 * SPEED[:, None] * SPEED[:, None], LANES, axis=1), F32)
    tile_spectra = pl.pallas_call(
        owner_kernel,
        out_shape=shape((OWN, NBINS, LANES), F32),
        in_specs=[SMEM_SPEC] + [VMEM_SPEC] * 2,
        out_specs=HBM_SPEC,
        scratch_shapes=[
            pltpu.VMEM((OWN, NBINS, LANES), F32),
            pltpu.VMEM((OWN, NFREQ, LANES), F32),
            pltpu.SemaphoreType.DMA((OWN,)),
        ],
        compiler_params=PARAMS,
        name="owned",
    )(slots, factor, got)

    other, tile_spectra = lax.optimization_barrier((other, tile_spectra))
    spectrum_next = pl.pallas_call(
        home_kernel,
        out_shape=shape((NDIR, ROWS, COLS), F32),
        in_specs=[SMEM_SPEC] + [VMEM_SPEC] * 3,
        out_specs=HBM_SPEC,
        scratch_shapes=[
            pltpu.VMEM((NDIR, ROWS, COLS), F32),
            pltpu.VMEM((LTILES, ROWS, LANES), F32),
            pltpu.SemaphoreType.DMA((4,)),
        ],
        compiler_params=PARAMS,
        name="home",
    )(at, grown, eights, other)
    return spectrum_next, tile_spectra


def solution(mesh):
    return jax.shard_map(
        shards,
        mesh=mesh,
        in_specs=(
            P("spec", "space", None),
            P("space", None),
            P("space", None),
            P("space", None),
            P("space", None),
            P("space", None),
            P(),
        ),
        out_specs=(P("spec", "space", None), P(("spec", "space"), None, None)),
        check_vma=False,
    )
```
